32 devices in a mesh: fsdp: 8 (over z, y), tp: 4 (over x, core).
Axes of the slice: x: 2, y: 2, z: 4, core: 2. Of those that a mesh axis runs over, the one named last changes fastest.
Arguments:
- residual: bfloat16 [4096, 2048], P(('fsdp', 'tp')), may hold values from -6 to 6
- segment_ids: int32 [8, 512], P('fsdp'), may hold values from 0 to 4, as said below
- qkv_weight: bfloat16 [3, 2048, 2048], P(None, 'fsdp', 'tp'), may hold values from -0.125 to 0.125
- qkv_bias: bfloat16 [2, 32, 64], P(None, 'tp', 'fsdp'), may hold values from -3 to 3
- out_weight: bfloat16 [2048, 2048], P('tp', 'fsdp'), may hold values from -1 to 1
- gate_up_weight: bfloat16 [2, 2048, 5632], P(None, 'fsdp', 'tp'), may hold values from -0.125 to 0.125
- down_weight: bfloat16 [5632, 2048], P('tp', 'fsdp'), may hold values from -0.078125 to 0.078125
- norm_gains: bfloat16 [2, 2048], P(None, 'fsdp'), may hold values from 0.5 to 1.5
- norm_biases: bfloat16 [2, 2048], P(None, 'fsdp'), may hold values from -2 to 2
- out_grad: bfloat16 [4096, 2048], P(('fsdp', 'tp')), may hold values from -6 to 6
Outputs:
- layer_out: bfloat16 [4096, 2048], P(('fsdp', 'tp'))
- input_grad: bfloat16 [4096, 2048], P(('fsdp', 'tp'))
- qkv_grad: float32 [3, 2048, 2048], P(None, 'fsdp', 'tp')
- qkv_bias_grad: float32 [2, 32, 64], P(None, 'tp', 'fsdp')
- out_weight_grad: float32 [2048, 2048], P('tp', 'fsdp')
- gate_up_grad: float32 [2, 2048, 5632], P(None, 'fsdp', 'tp')
- down_grad: float32 [5632, 2048], P('tp', 'fsdp')
- norm_gain_grad: float32 [2, 2048], P(None, 'fsdp')
- norm_bias_grad: float32 [2, 2048], P(None, 'fsdp')
The draws below stay inside these ranges and needn't reach their ends.
Inputs may be any that keep to these rules, and one draw needn't show every extreme that they name: `segment_ids`: along each group's 512 tokens segment numbers never fall. In every group one segment starts at a token index (counted from 0) of at most 32 and ends at a token index of at least 479.
All inputs are finite; a program needn't handle non-finite values.
Results may differ from the reference program's by a relative error of at most 0.014.
Values may be sent and summed in bfloat16 or wider, within the bound.
A program may use at most 256 MiB of HBM per device.

```python
import math
import jax
import jax.numpy as jnp
from jax import lax

D = 2048
HEADS = 32
HEAD = 64
ROT = 16
FF = 5632
TOK_DEV = 512
GROUPS = 8
TOKENS = 4096


def draw_segment_ids(key, part):
    key = jax.random.fold_in(key, 11)
    key_list = jax.random.split(key, 4)
    edge = TOK_DEV // 16
    begin_at = jax.random.randint(key_list[0], (GROUPS, 1), 1, edge + 1)
    first_cut = jax.random.randint(key_list[1], (GROUPS, 1), 0, 1 << 20) % begin_at + 1
    finish_at = jax.random.randint(key_list[2], (GROUPS, 1), TOK_DEV - edge, TOK_DEV)
    last_cut = finish_at + jax.random.randint(key_list[3], (GROUPS, 1), 0, 1 << 20) % (TOK_DEV - finish_at)
    positions = jnp.arange(TOK_DEV, dtype=jnp.int32)[None, :]
    numbers = (positions >= first_cut).astype(jnp.int32) + (positions >= begin_at).astype(jnp.int32)
    numbers = numbers + (positions >= finish_at).astype(jnp.int32) + (positions >= last_cut).astype(jnp.int32)
    return numbers.astype(jnp.int32)


def raised(values, own_key, source, target, shards_of, factor):
    def block_of(axis_at):
        return (jnp.arange(values.shape[axis_at]) // (values.shape[axis_at] // shards_of)).reshape((-1,) + (1,) * (values.ndim - 1 - axis_at))

    one_side = jax.random.permutation(own_key, shards_of)[block_of(target)]
    other_side = (block_of(target) + shards_of // 2) % shards_of
    return jnp.where((block_of(source) == one_side) | (block_of(source) == other_side), factor * values, values)


def level_of(own_key, extent, shards, smallest, high):
    factor_of = 1.0
    for dim, shards_of in shards:
        draws = jax.random.uniform(jax.random.fold_in(jax.random.fold_in(own_key, 6), dim), (shards_of,), jnp.float32, smallest / len(shards), high / len(shards))
        factor_of = factor_of * jnp.repeat(jnp.exp(draws), extent[dim] // shards_of).reshape((-1,) + (1,) * (len(extent) - 1 - dim))
    return factor_of


def gaussian(stream_key, extent, width, most, shards=(), kind=jnp.bfloat16):
    values = jax.random.normal(stream_key, extent, jnp.float32) * width
    if len(shards) > 0:
        values = level_of(stream_key, extent, shards, -0.22, 0.18) * values
    return jnp.clip(values, min=-most, max=most).astype(kind)


def bell_draw_with(stream_key, shape, scale, limit, cuts, heavy, kind=jnp.bfloat16):
    array = scale * jax.random.normal(stream_key, shape, jnp.float32)
    if cuts:
        array = array * level_of(stream_key, shape, cuts, -0.22, 0.18)
    return jnp.clip(raised(array, jax.random.fold_in(stream_key, 3), *heavy), -limit, limit).astype(kind)


def setup_inputs(seed: int = 0) -> dict:
    splits = jax.random.split(jax.random.key(seed), 11)
    return {
        "residual": gaussian(splits[0], (TOKENS, D), 1.0, 6.0, ((0, 32),)),
        "segment_ids": draw_segment_ids(jax.random.fold_in(splits[10], 71), 0),
        "qkv_weight": gaussian(splits[2], (3, D, D), D ** -0.5, 0.125, ((1, 8), (2, 4))),
        "qkv_bias": gaussian(splits[3], (2, HEADS, HEAD), 0.5, 3.0, ((1, 4), (2, 8))),
        "out_weight": gaussian(splits[4], (D, D), (D // 64) ** -0.5, 1.0, ((0, 4), (1, 8))),
        "gate_up_weight": gaussian(splits[5], (2, D, FF), D ** -0.5, 0.125, ((1, 8), (2, 4))),
        "down_weight": gaussian(splits[6], (FF, D), FF ** -0.5, 0.078125, ((0, 4), (1, 8))),
        "norm_gains": jnp.clip(1.0 + 0.1 * jax.random.normal(splits[7], (2, D), jnp.float32), 0.5, 1.5).astype(jnp.bfloat16),
        "norm_biases": gaussian(splits[8], (2, D), 0.3, 2.0, ((1, 8),)),
        "out_grad": bell_draw_with(splits[9], (TOKENS, D), 1.0, 6.0, ((0, 32),), (0, 1, 32, 2.75)),
    }


EPSILON = 1e-05
MASKED = -1e+30
ROPE_BASE = 10000.0
PRECISE = lax.Precision.HIGHEST

@jax.custom_vjp
def low(v):
    return lax.optimization_barrier(v.astype(jnp.bfloat16)).astype(jnp.float32)

@jax.custom_vjp
def low_back(v):
    return v

def low_keep(v):
    return (low(v), None)

def low_pass(kept, grad):
    return (grad,)

def back_keep(v):
    return (v, None)

def back_low(kept, grad):
    return (low(grad),)
low.defvjp(low_keep, low_pass)
low_back.defvjp(back_keep, back_low)

def layer_norm(values_in, gain, bias):
    average = lax.optimization_barrier(jnp.mean(values_in, axis=-1, keepdims=True))
    centred = values_in - average
    spread = lax.optimization_barrier(jnp.mean(centred * centred, axis=-1, keepdims=True))
    return centred * lax.rsqrt(spread + EPSILON) * gain + bias

def rotary_tables(segments):
    length = segments.shape[0]
    positions = jnp.arange(length, dtype=jnp.int32)
    starts_here = jnp.concatenate([jnp.ones((1,), jnp.bool_), segments[1:] != segments[:-1]])
    begins = lax.cummax(jnp.where(starts_here, positions, 0), axis=0)
    offsets = (positions - begins).astype(jnp.float32)
    half_rot = ROT // 2
    frequency = ROPE_BASE ** (-(jnp.arange(half_rot, dtype=jnp.float32) * 2.0 / ROT))
    angles = offsets[:, None] * frequency[None, :]
    cosine_table = jnp.concatenate([jnp.cos(angles), jnp.cos(angles)], axis=-1)
    sine_table = jnp.concatenate([jnp.sin(angles), jnp.sin(angles)], axis=-1)
    return (cosine_table, sine_table)

def rotate(head_vals, cosine_table, sine_table):
    half_rot = ROT // 2
    head_part = head_vals[..., :ROT]
    turned = jnp.concatenate([-head_part[..., half_rot:], head_part[..., :half_rot]], axis=-1)
    spun = head_part * cosine_table[:, None, :] + turned * sine_table[:, None, :]
    return jnp.concatenate([spun, head_vals[..., ROT:]], axis=-1)

def attend(queries, key_vals, values, segments):
    length = queries.shape[0]
    block_rows = min(512, length)
    blocks = length // block_rows
    positions = jnp.arange(length, dtype=jnp.int32)
    factor = 1.0 / math.sqrt(HEAD)

    def one_block(block_item):
        q_block, place_blk, seg_blk = block_item
        scores = jnp.einsum('bhe,she->hbs', q_block, key_vals, precision=PRECISE) * factor
        scores = low_back(scores)
        allowed = (seg_blk[:, None] == segments[None, :]) & (place_blk[:, None] >= positions[None, :])
        scores = jnp.where(allowed[None], scores, MASKED)
        highest = lax.optimization_barrier(jnp.max(scores, axis=-1, keepdims=True))
        weights = jnp.exp(scores - highest)
        attn_probs = low(weights / lax.optimization_barrier(jnp.sum(weights, axis=-1, keepdims=True)))
        return jnp.einsum('hbs,she->bhe', attn_probs, values, precision=PRECISE)
    outputs = lax.map(jax.checkpoint(one_block), (queries.reshape(blocks, block_rows, HEADS, HEAD), positions.reshape(blocks, block_rows), segments.reshape(blocks, block_rows)))
    return outputs.reshape(length, HEADS, HEAD)

def one_layer(group_rows, group_segs, params):
    qkv_w, qkv_b, out_w, gate_up_w, down_w, gains, biases = params
    length = group_rows.shape[0]
    cosine_table, sine_table = rotary_tables(group_segs)
    normed = low(layer_norm(group_rows, gains[0], biases[0]))
    bias_rows = qkv_b.reshape(2, D)
    full_bias = jnp.stack([bias_rows[0], jnp.zeros_like(bias_rows[0]), bias_rows[1]]).reshape(3, 1, D)
    projected = low_back(jnp.einsum('sd,cdf->csf', normed, qkv_w, precision=PRECISE) + full_bias)
    head_vals = projected.reshape(3, length, HEADS, HEAD)
    queries = low(rotate(head_vals[0], cosine_table, sine_table))
    key_vals = low(rotate(head_vals[1], cosine_table, sine_table))
    values = low(head_vals[2])
    mixed_out = attend(queries, key_vals, values, group_segs).reshape(length, D)
    mixed_out = low(low_back(mixed_out))
    branch = low_back(jnp.dot(mixed_out, out_w, precision=PRECISE))
    middle = group_rows + branch
    normed_two = low(layer_norm(middle, gains[1], biases[1]))
    gate_up = low_back(jnp.einsum('sd,cdf->csf', normed_two, gate_up_w, precision=PRECISE))
    hidden = low(jax.nn.silu(gate_up[0]) * gate_up[1])
    return middle + low_back(jnp.dot(hidden, down_w, precision=PRECISE))

def reference(residual, segment_ids, qkv_weight, qkv_bias, out_weight, gate_up_weight, down_weight, norm_gains, norm_biases, out_grad):
    stream = residual.astype(jnp.float32)
    params = (qkv_weight.astype(jnp.float32), qkv_bias.astype(jnp.float32), out_weight.astype(jnp.float32), gate_up_weight.astype(jnp.float32), down_weight.astype(jnp.float32), norm_gains.astype(jnp.float32), norm_biases.astype(jnp.float32))

    def forward(stream_in, params_in):

        def group_step(carry_in, block_item):
            group_rows, group_segs = block_item
            return (carry_in, one_layer(group_rows, group_segs, params_in))
        carry_zero = jnp.zeros((), jnp.float32)
        _, outputs = lax.scan(jax.checkpoint(group_step), carry_zero, (stream_in.reshape(GROUPS, TOK_DEV, D), segment_ids))
        return outputs.reshape(TOKENS, D)
    result, pullback = jax.vjp(forward, stream, params)
    grad_stream, grad_params = pullback(out_grad.astype(jnp.float32))
    return (result.astype(jnp.bfloat16), grad_stream.astype(jnp.bfloat16), grad_params[0], grad_params[1], grad_params[2], grad_params[3], grad_params[4], grad_params[5], grad_params[6])
```

```python
import functools
import math

import jax
import jax.numpy as jnp
from jax import lax
from jax.experimental import pallas as pl
from jax.experimental.pallas import tpu as pltpu
from jax.sharding import Mesh
from jax.sharding import PartitionSpec as P

HEAD = 64
ROT = 16
EPSILON = 1e-05
MASKED = -1e30
ROPE_BASE = 10000.0
F32 = jnp.float32
BF16 = jnp.bfloat16
MESH = pl.DeviceIdType.MESH


def norm_forward(values_in, gain, bias):
    average = jnp.mean(values_in, axis=-1, keepdims=True)
    centred = values_in - average
    factor = lax.rsqrt(jnp.mean(centred * centred, axis=-1, keepdims=True) + EPSILON)
    unit_rows = centred * factor
    return (unit_rows * gain + bias, unit_rows, factor)


def norm_backward(grad_rows, unit_rows, factor, gain):
    scaled = grad_rows * gain
    centred = scaled - jnp.mean(scaled, axis=-1, keepdims=True)
    back_rows = factor * (
        centred - unit_rows * jnp.mean(scaled * unit_rows, axis=-1, keepdims=True)
    )
    return (back_rows, jnp.sum(grad_rows * unit_rows, axis=0), jnp.sum(grad_rows, axis=0))


def rotary_tables(segments):
    length = segments.shape[0]
    positions = jnp.arange(length, dtype=jnp.int32)
    starts_here = jnp.concatenate([jnp.ones((1,), jnp.bool_), segments[1:] != segments[:-1]])
    begins = lax.cummax(jnp.where(starts_here, positions, 0), axis=0)
    offsets = (positions - begins).astype(F32)
    half_rot = ROT // 2
    frequency = ROPE_BASE ** (-(jnp.arange(half_rot, dtype=F32) * 2.0 / ROT))
    angles = offsets[:, None] * frequency[None, :]
    cosine_table = jnp.concatenate([jnp.cos(angles), jnp.cos(angles)], axis=-1)
    sine_table = jnp.concatenate([jnp.sin(angles), jnp.sin(angles)], axis=-1)
    return (cosine_table, sine_table)


def rotate(head_vals, cosine_table, sine_table):
    half_rot = ROT // 2
    head_part = head_vals[..., :ROT]
    turned = jnp.concatenate([-head_part[..., half_rot:], head_part[..., :half_rot]], axis=-1)
    spun = head_part * cosine_table[:, None, :] + turned * sine_table[:, None, :]
    return jnp.concatenate([spun, head_vals[..., ROT:]], axis=-1)


def unrotate(grad_vals, cosine_table, sine_table):
    half_rot = ROT // 2
    head_part = grad_vals[..., :ROT]
    with_sine = head_part * sine_table[:, None, :]
    back_turn = jnp.concatenate([with_sine[..., half_rot:], -with_sine[..., :half_rot]], axis=-1)
    spun = head_part * cosine_table[:, None, :] + back_turn
    return jnp.concatenate([spun, grad_vals[..., ROT:]], axis=-1)


def masked_scores(q, k, segments):
    factor = 1.0 / math.sqrt(HEAD)
    positions = jnp.arange(q.shape[1], dtype=jnp.int32)
    scores = jnp.einsum("gbhe,gshe->ghbs", q, k, preferred_element_type=F32) * factor
    allowed = (segments[:, :, None] == segments[:, None, :]) & (
        positions[:, None] >= positions[None, :]
    )
    return jnp.where(allowed[:, None], scores, MASKED)


def line_kernel(gather, count, lines, *refs):
    size, y, t, z = lines, lax.axis_index("y"), lax.axis_index("tp"), lax.axis_index("z")
    ins, outs = refs[:count], refs[count : 2 * count]
    send, recv, local = refs[2 * count :]
    barrier = pltpu.get_barrier_semaphore()
    for step in range(1, size):
        pl.semaphore_signal(
            barrier,
            inc=1,
            device_id=(lax.rem(z + step, size), y, t),
            device_id_type=MESH,
        )
    pl.semaphore_wait(barrier, size - 1)

    copies = []
    for m in range(count):
        for step in range(1, size):
            there = lax.rem(z + step, size)
            src = ins[m] if gather else slot(ins[m], there, size)
            dst = slot(outs[m], z, size) if gather else outs[m].at[z]
            copy = pltpu.make_async_remote_copy(
                src_ref=src,
                dst_ref=dst,
                send_sem=send.at[m, step - 1],
                recv_sem=recv.at[m, step - 1],
                device_id=(there, y, t),
                device_id_type=MESH,
            )
            copy.start()
            copies.append(copy)
        src = ins[m] if gather else slot(ins[m], z, size)
        dst = slot(outs[m], z, size) if gather else outs[m].at[z]
        copy = pltpu.make_async_copy(src, dst, local.at[m])
        copy.start()
        copies.append(copy)
    for copy in copies:
        copy.wait()


def slot(ref, index, size):
    width = ref.shape[1] // size
    return ref.at[:, pl.ds(pl.multiple_of(index * width, width), width)]


def line_call(gather, lines, arrays):
    count = len(arrays)

    def result(a):
        if gather:
            shape = list(a.shape)
            shape[1] *= lines
        else:
            shape = list(a.shape)
            shape[1] //= lines
            shape = [lines] + shape
        return jax.ShapeDtypeStruct(tuple(shape), a.dtype)

    return pl.pallas_call(
        functools.partial(line_kernel, gather, count, lines),
        out_shape=[result(a) for a in arrays],
        in_specs=[pl.BlockSpec(memory_space=pl.ANY)] * count,
        out_specs=[pl.BlockSpec(memory_space=pl.ANY)] * count,
        scratch_shapes=[
            pltpu.SemaphoreType.DMA((count, lines - 1)),
            pltpu.SemaphoreType.DMA((count, lines - 1)),
            pltpu.SemaphoreType.DMA((count,)),
        ],
        compiler_params=pltpu.CompilerParams(
            collective_id=1 if gather else 2, has_side_effects=True
        ),
    )(*arrays)


def swap_y(mine, other, y, axis):
    return jnp.where(
        y == 0,
        jnp.concatenate([mine, other], axis=axis),
        jnp.concatenate([other, mine], axis=axis),
    )


def exchange_y(halves, y):
    own = lax.dynamic_index_in_dim(halves, y, 0, keepdims=False)
    away = lax.dynamic_index_in_dim(halves, 1 - y, 0, keepdims=False)
    return own, lax.ppermute(away, "y", [(0, 1), (1, 0)])


def shards(
    lines,
    residual,
    segment_ids,
    qkv_weight,
    qkv_bias,
    out_weight,
    gate_up_weight,
    down_weight,
    norm_gains,
    norm_biases,
    out_grad,
):
    y = lax.axis_index("y")
    t = lax.axis_index("tp")
    z = lax.axis_index("z")
    plane = ("y", "tp")
    rows = qkv_weight.shape[1]
    width = rows * 2 * lines
    qc = qkv_weight.shape[2] // 2
    fc = gate_up_weight.shape[2] // 2
    heads = qc // HEAD
    own_rows = residual.shape[0]
    segments = lax.all_gather(segment_ids[0], "y", axis=0)
    length = segments.shape[1]
    tokens = 2 * length

    qkv_own, qkv_in = exchange_y(jnp.moveaxis(qkv_weight.reshape(3, rows, 2, qc), 2, 0), y)
    out_own, out_in = exchange_y(out_weight.reshape(2, qc, rows), y)
    gu_own, gu_in = exchange_y(jnp.moveaxis(gate_up_weight.reshape(2, rows, 2, fc), 2, 0), y)
    down_own, down_in = exchange_y(down_weight.reshape(2, fc, rows), y)
    qkv_full, out_full, gu_full, down_full = line_call(
        True,
        lines,
        [
            swap_y(qkv_own, qkv_in, y, 1),
            swap_y(out_own, out_in, y, 1),
            swap_y(gu_own, gu_in, y, 1),
            swap_y(down_own, down_in, y, 1),
        ],
    )
    small = jnp.concatenate([norm_gains, norm_biases], axis=0)
    small = lax.all_gather(small, ("z", "y"), axis=1, tiled=True).astype(F32)
    gains32, biases32 = small[:2], small[2:]
    bias_full = lax.all_gather(qkv_bias, ("z", "y"), axis=2, tiled=True).astype(F32)
    bias_own = lax.dynamic_slice_in_dim(bias_full, y * heads, heads, 1).reshape(2, qc)
    bias_three = jnp.stack([bias_own[0], jnp.zeros_like(bias_own[0]), bias_own[1]])

    tables = [jax.vmap(rotary_tables)(segments)][0]
    cos, sin = (v.reshape(tokens, ROT) for v in tables)
    stream = residual.astype(F32)
    normed, unit_one, factor_one = norm_forward(stream, gains32[0], biases32[0])
    normed_full = lax.all_gather(normed.astype(BF16), plane, axis=0, tiled=True)
    projected = [
        jnp.dot(normed_full, qkv_full[c], preferred_element_type=F32) + bias_three[c]
        for c in range(3)
    ]
    projected = [p.reshape(tokens, heads, HEAD) for p in projected]
    shape4 = (2, length, heads, HEAD)
    q = rotate(projected[0], cos, sin).astype(BF16).reshape(shape4)
    k = rotate(projected[1], cos, sin).astype(BF16).reshape(shape4)
    v = projected[2].astype(BF16).reshape(shape4)
    scores = masked_scores(q, k, segments)
    highest = jnp.max(scores, axis=-1, keepdims=True)
    weights = jnp.exp(scores - highest)
    denominator = jnp.sum(weights, axis=-1, keepdims=True)
    probs = (weights / denominator).astype(BF16)
    mixed = jnp.einsum("ghbs,gshe->gbhe", probs, v, preferred_element_type=F32).astype(BF16)
    log_totals = highest + jnp.log(denominator)
    mixed_flat = mixed.reshape(tokens, qc)
    middle = stream + lax.psum_scatter(
        jnp.dot(mixed_flat, out_full, preferred_element_type=F32),
        plane,
        scatter_dimension=0,
        tiled=True,
    )
    normed_two, unit_two, factor_two = norm_forward(middle, gains32[1], biases32[1])
    normed_two_full = lax.all_gather(normed_two.astype(BF16), plane, axis=0, tiled=True)
    gate_pre = jnp.dot(normed_two_full, gu_full[0], preferred_element_type=F32)
    up_pre = jnp.dot(normed_two_full, gu_full[1], preferred_element_type=F32)
    sigmoid_gate = jax.nn.sigmoid(gate_pre)
    hidden = (gate_pre * sigmoid_gate * up_pre).astype(BF16)
    layer_out = (
        middle
        + lax.psum_scatter(
            jnp.dot(hidden, down_full, preferred_element_type=F32),
            plane,
            scatter_dimension=0,
            tiled=True,
        )
    ).astype(BF16)
    grad_full = lax.all_gather(out_grad, plane, axis=0, tiled=True)
    nt = (((1,), (1,)), ((), ()))
    tn = (((0,), (0,)), ((), ()))
    grad_hidden = lax.dot_general(grad_full, down_full, nt, preferred_element_type=F32)
    grad_gate = grad_hidden * up_pre * sigmoid_gate * (1.0 + gate_pre * (1.0 - sigmoid_gate))
    grad_up = grad_hidden * gate_pre * sigmoid_gate
    grad_gate_up = [grad_gate.astype(BF16), grad_up.astype(BF16)]
    down_grad = lax.dot_general(hidden, grad_full, tn, preferred_element_type=F32)
    gate_up_grad = jnp.stack(
        [
            lax.dot_general(normed_two_full, g, tn, preferred_element_type=F32).astype(BF16)
            for g in grad_gate_up
        ]
    )
    grad_normed_two = lax.psum_scatter(
        lax.dot_general(grad_gate_up[0], gu_full[0], nt, preferred_element_type=F32)
        + lax.dot_general(grad_gate_up[1], gu_full[1], nt, preferred_element_type=F32),
        plane,
        scatter_dimension=0,
        tiled=True,
    )
    middle_part, gain_two, bias_two = norm_backward(
        grad_normed_two, unit_two, factor_two, gains32[1]
    )
    grad_middle = out_grad.astype(F32) + middle_part
    branch = lax.all_gather(grad_middle.astype(BF16), plane, axis=0, tiled=True)
    grad_mixed = lax.dot_general(branch, out_full, nt, preferred_element_type=F32)
    grad_mixed = grad_mixed.astype(BF16).reshape(shape4)
    out_weight_grad = lax.dot_general(mixed_flat, branch, tn, preferred_element_type=F32)
    scores = masked_scores(q, k, segments)
    probs32 = jnp.exp(scores - log_totals)
    dp = jnp.einsum("gbhe,gshe->ghbs", grad_mixed, v, preferred_element_type=F32)
    inner = jnp.sum(probs32 * dp, axis=-1, keepdims=True)
    grad_scores = (probs32 * (dp - inner)).astype(BF16)
    factor = 1.0 / math.sqrt(HEAD)
    gq = jnp.einsum("ghbs,gshe->gbhe", grad_scores, k, preferred_element_type=F32) * factor
    gk = jnp.einsum("ghbs,gbhe->gshe", grad_scores, q, preferred_element_type=F32) * factor
    gv = jnp.einsum(
        "ghbs,gbhe->gshe", probs32.astype(BF16), grad_mixed, preferred_element_type=F32
    )
    flat = (tokens, heads, HEAD)
    gp = [
        unrotate(gq.reshape(flat), cos, sin),
        unrotate(gk.reshape(flat), cos, sin),
        gv.reshape(flat),
    ]
    gp = [g.reshape(tokens, qc).astype(BF16) for g in gp]
    qkv_grad = jnp.stack(
        [lax.dot_general(normed_full, g, tn, preferred_element_type=F32).astype(BF16) for g in gp]
    )
    sums = jnp.stack([jnp.sum(gp[c].astype(F32), axis=0) for c in (0, 2)])
    grad_normed = sum(
        lax.dot_general(gp[c], qkv_full[c], nt, preferred_element_type=F32) for c in range(3)
    )
    grad_normed = lax.psum_scatter(grad_normed, plane, scatter_dimension=0, tiled=True)
    stream_part, gain_one, bias_one = norm_backward(grad_normed, unit_one, factor_one, gains32[0])
    input_grad = (grad_middle + stream_part).astype(BF16)

    parts = line_call(
        False,
        lines,
        [qkv_grad, out_weight_grad.astype(BF16), gate_up_grad, down_grad.astype(BF16)],
    )
    dq, do, dg, dd = (jnp.sum(p.astype(F32), axis=0) for p in parts)

    def finish(total, axis, column_axis):
        shape = total.shape
        halves = total.reshape(shape[:axis] + (2, shape[axis] // 2) + shape[axis + 1 :])
        own, came = exchange_y(jnp.moveaxis(halves, axis, 0), y)
        return swap_y(own, came, y, column_axis)

    qkv_out = finish(dq, 1, 2)
    out_out = finish(do, 1, 0)
    gu_out = finish(dg, 1, 2)
    down_out = finish(dd, 1, 0)
    vectors = jnp.stack([gain_one, gain_two, bias_one, bias_two])
    vectors = lax.psum(vectors, "tp")
    vectors = lax.psum_scatter(vectors, ("z", "y"), scatter_dimension=1, tiled=True)
    both = lax.dynamic_update_slice_in_dim(
        jnp.zeros((2, 2 * heads, HEAD), F32), sums.reshape(2, heads, HEAD), y * heads, 1
    )
    bias_out = lax.psum_scatter(both, ("z", "y"), scatter_dimension=2, tiled=True)
    return (
        layer_out,
        input_grad,
        qkv_out,
        bias_out,
        out_out,
        gu_out,
        down_out,
        vectors[:2],
        vectors[2:],
    )


def solution(mesh):
    groups, tp = mesh.shape["fsdp"], mesh.shape["tp"]
    lines = groups // 2
    cube = Mesh(mesh.devices.reshape(lines, 2, tp), ("z", "y", "tp"))
    fsdp = ("z", "y")
    token = P(("z", "y", "tp"), None)
    placed = (
        token,
        P(fsdp, None),
        P(None, fsdp, "tp"),
        P(None, "tp", fsdp),
        P("tp", fsdp),
        P(None, fsdp, "tp"),
        P("tp", fsdp),
        P(None, fsdp),
        P(None, fsdp),
        token,
    )
    return jax.shard_map(
        functools.partial(shards, lines),
        mesh=cube,
        in_specs=placed,
        out_specs=(
            token,
            token,
            P(None, fsdp, "tp"),
            P(None, "tp", fsdp),
            P("tp", fsdp),
            P(None, fsdp, "tp"),
            P("tp", fsdp),
            P(None, fsdp),
            P(None, fsdp),
        ),
        check_vma=False,
    )
```

```python
import functools
import math

import jax
import jax.numpy as jnp
from jax import lax
from jax.experimental import pallas as pl
from jax.experimental.pallas import tpu as pltpu
from jax.sharding import Mesh
from jax.sharding import PartitionSpec as P

HEAD = 64
ROT = 16
EPSILON = 1e-05
MASKED = -1e30
ROPE_BASE = 10000.0
F32 = jnp.float32
BF16 = jnp.bfloat16
MESH = pl.DeviceIdType.MESH
NN = (((1,), (0,)), ((), ()))
NT = (((1,), (1,)), ((), ()))
TN = (((0,), (0,)), ((), ()))
SCALE = 1.0 / math.sqrt(HEAD)


def dot(a, b, dims=NN):
    return lax.dot_general(a, b, dims, preferred_element_type=F32)


def tables(segments):
    length = segments.shape[0]
    positions = jnp.arange(length, dtype=jnp.int32)
    starts_here = jnp.concatenate([jnp.ones((1,), jnp.bool_), segments[1:] != segments[:-1]])
    begins = lax.cummax(jnp.where(starts_here, positions, 0), axis=0)
    offsets = (positions - begins).astype(F32)
    half_rot = ROT // 2
    frequency = ROPE_BASE ** (-(jnp.arange(half_rot, dtype=F32) * 2.0 / ROT))
    angles = offsets[:, None] * frequency[None, :]
    cos, sin = jnp.cos(angles), jnp.sin(angles)
    seg = segments.astype(F32)
    return jnp.concatenate(
        [
            cos,
            cos,
            jnp.ones((length, HEAD - ROT), F32),
            -sin,
            sin,
            jnp.zeros((length, 32 - ROT), F32),
            seg[:, None],
            jnp.zeros((length, 31), F32),
        ],
        axis=1,
    )


class Layer:
    def __init__(self, sizes, refs):
        self.__dict__.update(sizes)
        self.__dict__.update(refs)
        self.z, self.y, self.t = (lax.axis_index(a) for a in ("z", "y", "tp"))
        self.core = lax.rem(self.t, 2)
        self.x = lax.div(self.t, 2)
        self.sib = (self.z, self.y, self.t + 1 - 2 * self.core)
        self.xn = (self.z, self.y, lax.rem(self.t + 2, 4))
        self.yn = (self.z, 1 - self.y, self.t)
        self.sends = []

    def remote(self, src, dst, ssem, rsem, to):
        return pltpu.make_async_remote_copy(
            src_ref=src, dst_ref=dst, send_sem=ssem, recv_sem=rsem, device_id=to, device_id_type=MESH
        )

    def send(self, src, dst, ssem, rsem, to):
        copy = self.remote(src, dst, ssem, rsem, to)
        copy.start()
        self.sends.append(copy)

    def arrived(self, dst, rsem):
        self.remote(dst, dst, rsem, rsem, self.sib).wait_recv()

    def flush(self):
        for copy in self.sends:
            copy.wait_send()
        self.sends = []

    def chip_rows(self, y, x):
        return pl.multiple_of((y * 2 + x) * 2 * self.own, 2 * self.own)

    def chips(self):
        y, x = self.y, self.x
        return [
            self.chip_rows(1 - y, 1 - x),
            self.chip_rows(1 - y, x),
            self.chip_rows(y, 1 - x),
            self.chip_rows(y, x),
        ]

    def gather_start(self, u, buf):
        own, c = self.own, self.core
        mine = buf.at[pl.ds(pl.multiple_of(self.chips()[3] + c * own, own), own)]
        ss, rs = self.ag_send, self.ag_recv
        self.send(mine, mine, ss.at[u, 0], rs.at[u, 0], self.sib)
        self.send(mine, mine, ss.at[u, 1], rs.at[u, 1], self.xn)
        self.send(mine, mine, ss.at[u, 2], rs.at[u, 2], self.yn)

    def gather_relay(self, u, buf):
        own, c = self.own, self.core
        half = own // 2
        d, yr, xr, s = self.chips()
        ss, rs = self.ag_send, self.ag_recv

        def part(base, off, n):
            return buf.at[pl.ds(pl.multiple_of(base + c * own + off, half), n)]

        bx, by = part(xr, 0, own), part(yr, 0, own)
        self.arrived(bx, rs.at[u, 1])
        self.send(part(xr, 0, half), part(xr, 0, half), ss.at[u, 3], rs.at[u, 3], self.yn)
        self.send(bx, bx, ss.at[u, 4], rs.at[u, 4], self.sib)
        self.arrived(by, rs.at[u, 2])
        self.send(part(yr, half, half), part(yr, half, half), ss.at[u, 5], rs.at[u, 5], self.xn)
        self.send(by, by, ss.at[u, 6], rs.at[u, 6], self.sib)

    def gather_last(self, u, buf):
        own, c = self.own, self.core
        half = own // 2
        d = self.chips()[0]
        ss, rs = self.ag_send, self.ag_recv

        def part(off):
            return buf.at[pl.ds(pl.multiple_of(d + c * own + off, half), half)]

        self.arrived(part(0), rs.at[u, 3])
        self.send(part(0), part(0), ss.at[u, 7], rs.at[u, 7], self.sib)
        self.arrived(part(half), rs.at[u, 5])
        self.send(part(half), part(half), ss.at[u, 8], rs.at[u, 8], self.sib)

    def gather_wait(self, u, buf):
        own, c = self.own, self.core
        half = own // 2
        d, yr, xr, s = self.chips()
        rs = self.ag_recv

        def part(base, off, n):
            return buf.at[pl.ds(pl.multiple_of(base + (1 - c) * own + off, half), n)]

        self.arrived(part(s, 0, own), rs.at[u, 0])
        self.arrived(part(xr, 0, own), rs.at[u, 4])
        self.arrived(part(yr, 0, own), rs.at[u, 6])
        self.arrived(part(d, 0, half), rs.at[u, 7])
        self.arrived(part(d, half, half), rs.at[u, 8])

    def reduce_start(self, u, compute):
        own, c = self.own, self.core
        for j, row in enumerate(self.chips()):
            compute(j, row)
            there = pl.ds(pl.multiple_of(j * 2 * own + (1 - c) * own, own), own)
            if u >= 1:
                pass
            self.csend[j] = self.fbig[there, :].astype(BF16)
            self.send(
                self.csend.at[j], self.crecv.at[j], self.rs_send.at[u, j], self.rs_recv.at[u, j], self.sib
            )

    def reduce_mine(self, j):
        own, c = self.own, self.core
        return self.fbig[pl.ds(pl.multiple_of(j * 2 * own + c * own, own), own), :]

    def reduce_relay(self, u):
        own, half = self.own, self.own // 2
        ss, rs = self.rs_send, self.rs_recv
        self.arrived(self.crecv.at[0], rs.at[u, 0])
        self.hsend[0] = (self.reduce_mine(0) + self.crecv[0].astype(F32)).astype(BF16)
        first, second = pl.ds(0, half), pl.ds(half, half)
        self.send(self.hsend.at[0, first], self.dvia.at[0], ss.at[u, 4], rs.at[u, 4], self.xn)
        self.send(self.hsend.at[0, second], self.dvia.at[1], ss.at[u, 5], rs.at[u, 5], self.yn)
        for j, rows, to in ((1, (0, half), self.yn), (2, (half, own), self.xn)):
            self.arrived(self.crecv.at[j], rs.at[u, j])
            total = self.reduce_mine(j) + self.crecv[j].astype(F32)
            self.fbig[pl.ds(j * 2 * own, own), :] = total
            self.arrived(self.dvia.at[j - 1], rs.at[u, 3 + j])
            add = self.dvia[j - 1].astype(F32)
            lo, hi = rows
            self.fbig[pl.ds(j * 2 * own + lo, half), :] = total[lo:hi] + add
            self.hsend[j] = self.fbig[pl.ds(j * 2 * own, own), :].astype(BF16)
            self.send(self.hsend.at[j], self.hrecv.at[j - 1], ss.at[u, 5 + j], rs.at[u, 5 + j], to)

    def reduce_finish(self, u):
        rs = self.rs_recv
        self.arrived(self.crecv.at[3], rs.at[u, 3])
        total = self.reduce_mine(3) + self.crecv[3].astype(F32)
        self.arrived(self.hrecv.at[0], rs.at[u, 6])
        total = total + self.hrecv[0].astype(F32)
        self.arrived(self.hrecv.at[1], rs.at[u, 7])
        return total + self.hrecv[1].astype(F32)

    def item(self, m, zz):
        rows = pl.ds(pl.multiple_of(zz * self.depth, self.depth), self.depth)
        if m == 0:
            return self.wq.at[:, rows]
        if m == 1:
            return self.wo.at[zz]
        if m in (2, 3):
            return self.wg.at[m - 2, rows]
        return self.wd.at[zz]

    def line_start(self, m):
        z, n = self.z, self.lines
        for step in range(1, n):
            to = lax.rem(z + step, n)

            def go(to=to, step=step):
                self.remote(
                    self.item(m, z),
                    self.item(m, z),
                    self.z_send.at[m, step],
                    self.z_recv.at[m, z],
                    (to, self.y, self.t),
                ).start()

            if n == 4 and step in (1, 3):
                pl.when(self.straight(step))(go)
            else:
                go()

    def straight(self, step):
        return jnp.logical_not((self.z == 3) if step == 1 else (self.z == 0))

    def line_flush(self, m):
        z, n = self.z, self.lines
        for step in range(1, n):

            def done(step=step):
                self.remote(
                    self.item(m, z),
                    self.item(m, z),
                    self.z_send.at[m, step],
                    self.z_recv.at[m, z],
                    (z, self.y, self.t),
                ).wait_send()

            if n == 4 and step in (1, 3):
                pl.when(self.straight(step))(done)
            else:
                done()
        if n == 4:

            @pl.when((z == 1) | (z == 2))
            def _():
                far = jnp.where(z == 1, 3, 0)
                self.remote(
                    self.item(m, far),
                    self.item(m, far),
                    self.z_send.at[m, 0],
                    self.z_recv.at[m, far],
                    (z, self.y, self.t),
                ).wait_send()

    def line_order(self, s):
        z, n = self.z, self.lines
        if n != 4:
            return lax.rem(z + s, n)
        low = z < 2
        if s == 0:
            return z
        if s == 1:
            return z + 1 - 2 * lax.rem(z, 2)
        if s == 2:
            return jnp.where(low, 2, 1)
        return jnp.where(low, 3, 0)

    def line_wait(self, m, s):
        zz = self.line_order(s)
        if s == 0:
            return zz
        self.arrived(self.item(m, zz), self.z_recv.at[m, zz])
        if self.lines == 4 and s == 3:
            z = self.z

            @pl.when((z == 1) | (z == 2))
            def _():
                self.remote(
                    self.item(m, zz),
                    self.item(m, zz),
                    self.z_send.at[m, 0],
                    self.z_recv.at[m, zz],
                    (3 * (z - 1), self.y, self.t),
                ).start()

        return zz

    def enter(self):
        z, y, t = self.z, self.y, self.t
        barrier = pltpu.get_barrier_semaphore()
        n = 2 * self.lines
        f = z * 2 + y
        others = []
        for step in range(1, n):
            g = lax.rem(f + step, n)
            others.append((lax.div(g, 2), lax.rem(g, 2), t))
        for to in others + [self.sib, self.xn]:
            pl.semaphore_signal(barrier, inc=1, device_id=to, device_id_type=MESH)
        pl.semaphore_wait(barrier, n + 1)
        return f, others

    def unit_rows(self, rows):
        mean = jnp.mean(rows, axis=-1, keepdims=True)
        centred = rows - mean
        factor = lax.rsqrt(jnp.mean(centred * centred, axis=-1, keepdims=True) + EPSILON)
        return centred * factor, factor

    def rope_tables(self, g):
        rows = pl.ds(pl.multiple_of(g * self.length, self.length), self.length)
        both = self.tab[rows, :]
        lane = lax.broadcasted_iota(jnp.int32, both.shape, 1)
        turned = pltpu.roll(both, 64, 1)
        cos = jnp.where(lane < 64, both, turned)
        sin = jnp.where(lane < 64, turned, both)
        dim = lax.rem(lane, HEAD)
        seg = self.tab[rows, 96:97]
        return cos, jnp.where(dim < ROT, sin, 0.0), dim, seg

    def turn(self, v, dim):
        ahead = pltpu.roll(v, 128 - ROT // 2, 1)
        behind = pltpu.roll(v, ROT // 2, 1)
        return jnp.where(dim < ROT // 2, ahead, jnp.where(dim < ROT, behind, 0.0))

    def masked(self, scores, seg, g, r0):
        rows, cols = scores.shape
        at = lax.broadcasted_iota(jnp.int32, scores.shape, 0) + r0
        key = lax.broadcasted_iota(jnp.int32, scores.shape, 1)
        seg_row = self.segrow[g, 0:1, 0:cols]
        return jnp.where((seg == seg_row) & (at >= key), scores * SCALE, MASKED)


def forward(k):
    own, length, tokens = k.own, k.length, 2 * k.length
    width, rows_f, depth = k.width, k.rows, k.depth
    c, y = k.core, k.y
    f, others = k.enter()
    loads = k.loads
    for i, (src, dst) in enumerate(
        (
            (k.in_gu, k.gu_raw),
            (k.in_qkv.at[:, :, pl.ds(pl.multiple_of(y * k.qc, k.qc), k.qc)],
             k.wq.at[:, pl.ds(pl.multiple_of(f * rows_f, rows_f), rows_f)]),
            (k.in_out.at[pl.ds(pl.multiple_of(y * k.qc, k.qc), k.qc)], k.sout.at[y]),
            (k.in_down.at[pl.ds(pl.multiple_of(y * k.fc, 16), k.fc)], k.sdown.at[y]),
        )
    ):
        pltpu.make_async_copy(src, dst, loads.at[i]).start()
    k.small[f] = k.in_small[...]
    for i, to in enumerate(others):
        k.send(k.in_small, k.small.at[f], k.sm_send.at[i], k.sm_recv.at[f], to)
    mine = pl.ds(pl.multiple_of(y * length, length), length)
    k.tab[mine, :] = k.in_tab[...]
    k.segrow[y] = k.in_seg[...]
    k.send(k.in_tab, k.tab.at[mine], k.yx_send.at[0], k.yx_recv.at[0], k.yn)
    k.send(k.in_seg, k.segrow.at[y], k.yx_send.at[1], k.yx_recv.at[1], k.yn)
    away = 1 - y
    frows = pl.ds(pl.multiple_of(f * rows_f, rows_f), rows_f)
    k.send(
        k.in_qkv.at[:, :, pl.ds(pl.multiple_of(away * k.qc, k.qc), k.qc)],
        k.wq.at[:, frows],
        k.yx_send.at[2], k.yx_recv.at[2], k.yn,
    )
    k.send(
        k.in_out.at[pl.ds(pl.multiple_of(away * k.qc, k.qc), k.qc)],
        k.sout.at[y],
        k.yx_send.at[3], k.yx_recv.at[3], k.yn,
    )
    unit, _ = k.unit_rows(k.in_res[...].astype(F32))
    pltpu.make_async_copy(k.in_gu, k.gu_raw, loads.at[0]).wait()
    for i in range(2):
        low, high = k.gu_raw[i, :, 0 : k.fc], k.gu_raw[i, :, k.fc : 2 * k.fc]
        k.wg[i, frows, :] = jnp.where(y == 0, low, high)
        k.gu_away[i] = jnp.where(y == 0, high, low)
        k.send(
            k.gu_away.at[i], k.wg.at[i, frows], k.yx_send.at[4 + i], k.yx_recv.at[4 + i], k.yn
        )
    k.send(
        k.in_down.at[pl.ds(pl.multiple_of(away * k.fc, 16), k.fc)],
        k.sdown.at[y],
        k.yx_send.at[6], k.yx_recv.at[6], k.yn,
    )
    for step in range(1, len(others) + 1):
        g = lax.rem(f + step, len(others) + 1)
        k.arrived(k.small.at[g], k.sm_recv.at[g])
    for g in range(len(others) + 1):
        k.gains[:, g * rows_f : (g + 1) * rows_f] = k.small[g, 0:4, 0:rows_f]
    bias = k.small[0, 4:6, :]
    for g in range(1, len(others) + 1):
        bias = bias + k.small[g, 4:6, :]
    bias = jnp.where(y == 0, bias[:, 0 : k.qc], bias[:, k.qc : 2 * k.qc])
    at = k.chips()[3] + c * own
    mine_rows = pl.ds(pl.multiple_of(at, own), own)
    k.h1[mine_rows, :] = (unit * k.gains[0:1, :] + k.gains[2:3, :]).astype(BF16)
    k.gather_start(0, k.h1)

    pltpu.make_async_copy(k.in_qkv.at[:, :, pl.ds(0, k.qc)], k.wq.at[:, frows], loads.at[1]).wait()
    nrows = pl.ds(pl.multiple_of((f + 1 - 2 * y) * rows_f, rows_f), rows_f)
    k.arrived(k.wq.at[:, nrows], k.yx_recv.at[2])
    k.line_start(0)
    pltpu.make_async_copy(k.in_out.at[pl.ds(0, k.qc)], k.sout.at[0], loads.at[2]).wait()
    k.arrived(k.sout.at[away], k.yx_recv.at[3])
    k.wo[k.z] = jnp.concatenate([k.sout[0], k.sout[1]], axis=1)
    k.line_start(1)
    k.gather_relay(0, k.h1)
    for i in range(2):
        k.arrived(k.wg.at[i, nrows], k.yx_recv.at[4 + i])
        k.line_start(2 + i)
    pltpu.make_async_copy(k.in_down.at[pl.ds(0, k.fc)], k.sdown.at[0], loads.at[3]).wait()
    k.arrived(k.sdown.at[away], k.yx_recv.at[6])
    k.wd[k.z] = jnp.concatenate([k.sdown[0], k.sdown[1]], axis=1)
    k.line_start(4)
    k.gather_last(0, k.h1)
    k.arrived(k.tab.at[pl.ds(pl.multiple_of(away * length, length), length)], k.yx_recv.at[0])
    k.arrived(k.segrow.at[away], k.yx_recv.at[1])
    k.gather_wait(0, k.h1)
    k.og[mine_rows, :] = k.in_og[...]
    k.gather_start(1, k.og)

    tile = 256
    for s in range(k.lines):
        zz = k.line_wait(0, s)
        cols = pl.ds(pl.multiple_of(zz * depth, depth), depth)

        @pl.loop(0, tokens // tile)
        def _(i):
            rows = pl.ds(pl.multiple_of(i * tile, tile), tile)
            a = k.h1[rows, cols]
            for j in range(3):
                out = dot(a, k.wq[j, cols, :])
                into = pl.ds(j * k.qc, k.qc)
                if s == 0:
                    k.fbig[rows, into] = out
                else:
                    k.fbig[rows, into] += out

    k.gather_relay(1, k.og)

    pairs = k.qc // 128
    block = 256

    @pl.loop(0, 2)
    def _(g):
        rows = pl.ds(pl.multiple_of(g * length, length), length)
        cos, sin, dim, seg = k.rope_tables(g)
        lane = lax.broadcasted_iota(jnp.int32, (length, 128), 1)
        lse = jnp.zeros((length, 128), F32)
        for p in range(pairs):
            into = pl.ds(p * 128, 128)

            def part(j):
                return k.fbig[rows, pl.ds(j * k.qc + p * 128, 128)]

            q = part(0) + bias[0:1, p * 128 : (p + 1) * 128]
            kk = part(1)
            k.qkv[0, rows, into] = (q * cos + k.turn(q, dim) * sin).astype(BF16)
            k.qkv[1, rows, into] = (kk * cos + k.turn(kk, dim) * sin).astype(BF16)
            k.qkv[2, rows, into] = (part(2) + bias[1:2, p * 128 : (p + 1) * 128]).astype(BF16)
            for r in range(0, length, block):
                some = pl.ds(pl.multiple_of(g * length + r, block), block)
                seen = pl.ds(pl.multiple_of(g * length, length), r + block)
                qb = k.qkv[0, some, into]
                kb = k.qkv[1, seen, into]
                vb = k.qkv[2, seen, into]
                low = lax.broadcasted_iota(jnp.int32, (block, 128), 1) < HEAD
                both = []
                marks = []
                for h in range(2):
                    mask = low if h == 0 else jnp.logical_not(low)
                    scores = dot(jnp.where(mask, qb, jnp.zeros_like(qb)), kb, NT)
                    scores = k.masked(scores, seg[r : r + block], g, r)
                    top = jnp.max(scores, axis=-1, keepdims=True)
                    e = jnp.exp(scores - top)
                    total = jnp.sum(e, axis=-1, keepdims=True)
                    probs = (e / total).astype(BF16)
                    both.append(dot(probs, vb))
                    marks.append(top + jnp.log(total))
                k.mixed[some, into] = jnp.where(low, both[0], both[1]).astype(BF16)
                at_lane = lax.broadcasted_iota(jnp.int32, (block, 128), 1)
                old = k.lse[some, :]
                old = jnp.where(at_lane == 2 * p, marks[0], old)
                k.lse[some, :] = jnp.where(at_lane == 2 * p + 1, marks[1], old)

    k.gather_last(1, k.og)
    for s in range(k.lines):
        k.line_wait(1, s)

    def project(j, row):
        a = k.mixed[pl.ds(row, 2 * own), :]
        for zz in range(k.lines):
            k.fbig[j * 2 * own : (j + 1) * 2 * own, zz * depth : (zz + 1) * depth] = dot(a, k.wo[zz])

    k.reduce_start(0, project)
    k.reduce_relay(0)
    middle = k.in_res[...].astype(F32) + k.reduce_finish(0)
    k.middle[...] = middle
    unit, _ = k.unit_rows(middle)
    k.h2[mine_rows, :] = (unit * k.gains[1:2, :] + k.gains[3:4, :]).astype(BF16)
    k.gather_start(2, k.h2)
    k.gather_wait(1, k.og)
    k.gather_relay(2, k.h2)
    k.gather_last(2, k.h2)
    k.gather_wait(2, k.h2)

    for i in range(2):
        for s in range(k.lines):
            zz = k.line_wait(2 + i, s)
            cols = pl.ds(pl.multiple_of(zz * depth, depth), depth)

            @pl.loop(0, tokens // tile)
            def _(n):
                rows = pl.ds(pl.multiple_of(n * tile, tile), tile)
                out = dot(k.h2[rows, cols], k.wg[i, cols, :])
                into = pl.ds(i * k.fpad, k.fc)
                if s == 0:
                    k.fbig[rows, into] = out
                else:
                    k.fbig[rows, into] += out

    @pl.loop(0, tokens // 64)
    def _(n):
        rows = pl.ds(pl.multiple_of(n * 64, 64), 64)
        gate = k.fbig[rows, 0 : k.fc]
        up = k.fbig[rows, k.fpad : k.fpad + k.fc]
        sig = 1.0 / (1.0 + jnp.exp(-gate))
        silu = gate * sig
        k.hidden[rows, :] = (silu * up).astype(BF16)
        k.by_gate[rows, :] = (up * sig * (1.0 + gate * (1.0 - sig))).astype(BF16)
        k.by_up[rows, :] = silu.astype(BF16)


def kernel(names, sizes, *refs):
    k = Layer(sizes, dict(zip(names, refs)))
    forward(k)
    own = k.own
    for s in range(k.lines):
        k.line_wait(4, s)
    depth = k.depth

    def feed(j, row):
        a = k.hidden[pl.ds(row, 2 * own), :]
        for zz in range(k.lines):
            k.fbig[j * 2 * own : (j + 1) * 2 * own, zz * depth : (zz + 1) * depth] = dot(a, k.wd[zz])

    k.flush()
    k.reduce_start(1, feed)
    k.reduce_relay(1)
    k.o_layer[...] = (k.middle[...] + k.reduce_finish(1)).astype(BF16)
    k.flush()
    for m in range(5):
        k.line_flush(m)
    outs = []
    for i, name in enumerate(EXPORT):
        copy = pltpu.make_async_copy(getattr(k, name), getattr(k, "o_" + name), k.stores.at[i])
        copy.start()
        outs.append(copy)
    for copy in outs:
        copy.wait()


EXPORT = ("wq", "wo", "wg", "wd", "h1", "h2", "og", "qkv", "mixed", "lse", "hidden", "by_gate", "by_up", "middle", "gains")


def layer_call(sizes, inputs):
    s = sizes
    lines, width, own, qc, fc, rows, depth = (
        s[n] for n in ("lines", "width", "own", "qc", "fc", "rows", "depth")
    )
    tokens = 2 * s["length"]
    groups = 2 * lines
    vm = dict(
        wq=((3, width, qc), BF16),
        wo=((lines, qc, depth), BF16),
        wg=((2, width, fc), BF16),
        wd=((lines, fc, depth), BF16),
        h1=((tokens, width), BF16),
        h2=((tokens, width), BF16),
        og=((tokens, width), BF16),
        qkv=((3, tokens, qc), BF16),
        mixed=((tokens, qc), BF16),
        lse=((tokens, 128), F32),
        hidden=((tokens, fc), BF16),
        by_gate=((tokens, fc), BF16),
        by_up=((tokens, fc), BF16),
        middle=((own, width), F32),
        gains=((4, width), F32),
        fbig=((tokens, width), F32),
        csend=((4, own, width), BF16),
        crecv=((4, own, width), BF16),
        hsend=((3, own, width), BF16),
        hrecv=((2, own, width), BF16),
        dvia=((2, own // 2, width), BF16),
        gu_raw=((2, rows, 2 * fc), BF16),
        gu_away=((2, rows, fc), BF16),
        sout=((2, qc, rows), BF16),
        sdown=((2, fc, rows), BF16),
        small=((groups, 8, 2 * qc), F32),
        tab=((tokens, 128), F32),
        segrow=((2, 8, s["length"]), F32),
    )
    sems = dict(
        ag_send=(4, 9),
        ag_recv=(4, 9),
        rs_send=(4, 8),
        rs_recv=(4, 8),
        z_send=(5, lines),
        z_recv=(5, lines),
        yx_send=(7,),
        yx_recv=(7,),
        sm_send=(groups - 1,),
        sm_recv=(groups,),
        loads=(4,),
        stores=(len(EXPORT),),
    )
    outs = {"o_layer": ((own, width), BF16, pltpu.VMEM)}
    for name in EXPORT:
        outs["o_" + name] = vm[name] + (pl.ANY,)
    in_vm = ("in_res", "in_og", "in_tab", "in_seg", "in_small")
    names = list(inputs) + list(outs) + list(vm) + list(sems)
    results = pl.pallas_call(
        functools.partial(kernel, names, sizes),
        out_shape=[jax.ShapeDtypeStruct(a, d) for a, d, _ in outs.values()],
        in_specs=[
            pl.BlockSpec(memory_space=pltpu.VMEM if n in in_vm else pl.ANY) for n in inputs
        ],
        out_specs=[pl.BlockSpec(memory_space=m) for _, _, m in outs.values()],
        scratch_shapes=[pltpu.VMEM(*v) for v in vm.values()]
        + [pltpu.SemaphoreType.DMA(v) for v in sems.values()],
        compiler_params=pltpu.CompilerParams(
            collective_id=1, has_side_effects=True, vmem_limit_bytes=63 * 2**20
        ),
    )(*inputs.values())
    return dict(zip([n[2:] for n in outs], results))


def norm_forward(values_in, gain, bias):
    average = jnp.mean(values_in, axis=-1, keepdims=True)
    centred = values_in - average
    factor = lax.rsqrt(jnp.mean(centred * centred, axis=-1, keepdims=True) + EPSILON)
    unit_rows = centred * factor
    return (unit_rows * gain + bias, unit_rows, factor)


def norm_backward(grad_rows, unit_rows, factor, gain):
    scaled = grad_rows * gain
    centred = scaled - jnp.mean(scaled, axis=-1, keepdims=True)
    back_rows = factor * (
        centred - unit_rows * jnp.mean(scaled * unit_rows, axis=-1, keepdims=True)
    )
    return (back_rows, jnp.sum(grad_rows * unit_rows, axis=0), jnp.sum(grad_rows, axis=0))


def unrotate(grad_vals, cosine_table, sine_table):
    half_rot = ROT // 2
    head_part = grad_vals[..., :ROT]
    with_sine = head_part * sine_table[:, None, :]
    back_turn = jnp.concatenate([with_sine[..., half_rot:], -with_sine[..., :half_rot]], axis=-1)
    spun = head_part * cosine_table[:, None, :] + back_turn
    return jnp.concatenate([spun, grad_vals[..., ROT:]], axis=-1)


def masked_scores(q, k, segments):
    factor = 1.0 / math.sqrt(HEAD)
    positions = jnp.arange(q.shape[1], dtype=jnp.int32)
    scores = jnp.einsum("gbhe,gshe->ghbs", q, k, preferred_element_type=F32) * factor
    allowed = (segments[:, :, None] == segments[:, None, :]) & (
        positions[:, None] >= positions[None, :]
    )
    return jnp.where(allowed[:, None], scores, MASKED)


def line_kernel(gather, count, lines, *refs):
    size, y, t, z = lines, lax.axis_index("y"), lax.axis_index("tp"), lax.axis_index("z")
    ins, outs = refs[:count], refs[count : 2 * count]
    send, recv, local = refs[2 * count :]
    barrier = pltpu.get_barrier_semaphore()
    for step in range(1, size):
        pl.semaphore_signal(
            barrier,
            inc=1,
            device_id=(lax.rem(z + step, size), y, t),
            device_id_type=MESH,
        )
    pl.semaphore_wait(barrier, size - 1)

    copies = []
    for m in range(count):
        for step in range(1, size):
            there = lax.rem(z + step, size)
            src = ins[m] if gather else slot(ins[m], there, size)
            dst = slot(outs[m], z, size) if gather else outs[m].at[z]
            copy = pltpu.make_async_remote_copy(
                src_ref=src,
                dst_ref=dst,
                send_sem=send.at[m, step - 1],
                recv_sem=recv.at[m, step - 1],
                device_id=(there, y, t),
                device_id_type=MESH,
            )
            copy.start()
            copies.append(copy)
        src = ins[m] if gather else slot(ins[m], z, size)
        dst = slot(outs[m], z, size) if gather else outs[m].at[z]
        copy = pltpu.make_async_copy(src, dst, local.at[m])
        copy.start()
        copies.append(copy)
    for copy in copies:
        copy.wait()


def slot(ref, index, size):
    width = ref.shape[1] // size
    return ref.at[:, pl.ds(pl.multiple_of(index * width, width), width)]


def line_call(gather, lines, arrays):
    count = len(arrays)

    def result(a):
        if gather:
            shape = list(a.shape)
            shape[1] *= lines
        else:
            shape = list(a.shape)
            shape[1] //= lines
            shape = [lines] + shape
        return jax.ShapeDtypeStruct(tuple(shape), a.dtype)

    return pl.pallas_call(
        functools.partial(line_kernel, gather, count, lines),
        out_shape=[result(a) for a in arrays],
        in_specs=[pl.BlockSpec(memory_space=pl.ANY)] * count,
        out_specs=[pl.BlockSpec(memory_space=pl.ANY)] * count,
        scratch_shapes=[
            pltpu.SemaphoreType.DMA((count, lines - 1)),
            pltpu.SemaphoreType.DMA((count, lines - 1)),
            pltpu.SemaphoreType.DMA((count,)),
        ],
        compiler_params=pltpu.CompilerParams(
            collective_id=2, has_side_effects=True
        ),
    )(*arrays)


def swap_y(mine, other, y, axis):
    return jnp.where(
        y == 0,
        jnp.concatenate([mine, other], axis=axis),
        jnp.concatenate([other, mine], axis=axis),
    )


def exchange_y(halves, y):
    own = lax.dynamic_index_in_dim(halves, y, 0, keepdims=False)
    away = lax.dynamic_index_in_dim(halves, 1 - y, 0, keepdims=False)
    return own, lax.ppermute(away, "y", [(0, 1), (1, 0)])


def prepare(lines, segment_ids, qkv_weight, qkv_bias, norm_gains, norm_biases):
    groups = 2 * lines
    f = lax.axis_index("z") * 2 + lax.axis_index("y")
    segments = segment_ids[0]
    table = tables(segments)
    seg_row = jnp.broadcast_to(segments.astype(F32)[None, :], (8, segments.shape[0]))
    width = qkv_weight.shape[2]
    two, heads, dims = qkv_bias.shape
    placed = lax.dynamic_update_slice(
        jnp.zeros((two, heads, groups, dims), F32), qkv_bias.astype(F32)[:, :, None, :], (0, 0, f, 0)
    ).reshape(two, width)
    params = jnp.concatenate([norm_gains, norm_biases], axis=0).astype(F32)
    params = jnp.pad(params, ((0, 0), (0, width - params.shape[1])))
    small = jnp.concatenate([params, placed, jnp.zeros((2, width), F32)], axis=0)
    return table, seg_row, small


def shards(
    lines,
    residual,
    segment_ids,
    qkv_weight,
    qkv_bias,
    out_weight,
    gate_up_weight,
    down_weight,
    norm_gains,
    norm_biases,
    out_grad,
):
    y = lax.axis_index("y")
    plane = ("y", "tp")
    rows = qkv_weight.shape[1]
    qc = qkv_weight.shape[2] // 2
    fc = gate_up_weight.shape[2] // 2
    length = segment_ids.shape[1]
    table, seg_row, small = prepare(
        lines, segment_ids, qkv_weight, qkv_bias, norm_gains, norm_biases
    )
    sizes = dict(
        lines=lines,
        own=residual.shape[0],
        length=length,
        width=residual.shape[1],
        rows=rows,
        depth=2 * rows,
        qc=qc,
        fc=fc,
        fpad=-(-fc // 128) * 128,
    )
    r = layer_call(
        sizes,
        dict(
            in_res=residual,
            in_og=out_grad,
            in_tab=table,
            in_seg=seg_row,
            in_small=small,
            in_qkv=qkv_weight,
            in_out=out_weight,
            in_gu=gate_up_weight,
            in_down=down_weight,
        ),
    )
    heads = qc // HEAD
    tokens = 2 * length
    qkv_full, gu_full = r["wq"], r["wg"]
    out_full = jnp.moveaxis(r["wo"], 0, 1).reshape(qc, -1)
    down_full = jnp.moveaxis(r["wd"], 0, 1).reshape(fc, -1)
    gains32 = r["gains"][:2]
    segments = lax.all_gather(segment_ids[0], "y", axis=0)
    tabs = jax.vmap(tables)(segments).reshape(tokens, 128)
    cos = tabs[:, :ROT]
    sin = jnp.concatenate([tabs[:, 64 + 8 : 64 + 16]] * 2, axis=1)
    shape4 = (2, length, heads, HEAD)
    q, kk, v = (r["qkv"][c].reshape(shape4) for c in range(3))
    log_totals = jnp.transpose(r["lse"][:, :heads].reshape(2, length, heads), (0, 2, 1))[..., None]
    mixed_flat = r["mixed"]
    stream = residual.astype(F32)
    normed, unit_one, factor_one = norm_forward(stream, gains32[0], r["gains"][2])
    normed_full, normed_two_full, grad_full = r["h1"], r["h2"], r["og"]
    middle = r["middle"]
    normed_two, unit_two, factor_two = norm_forward(middle, gains32[1], r["gains"][3])
    hidden = r["hidden"]
    grad_hidden = lax.dot_general(grad_full, down_full, NT, preferred_element_type=F32)
    grad_gate_up = [
        (grad_hidden * r["by_gate"].astype(F32)).astype(BF16),
        (grad_hidden * r["by_up"].astype(F32)).astype(BF16),
    ]
    nt, tn = NT, TN
    layer_out = r["layer"]
    down_grad = lax.dot_general(hidden, grad_full, tn, preferred_element_type=F32)
    gate_up_grad = jnp.stack(
        [
            lax.dot_general(normed_two_full, g, tn, preferred_element_type=F32).astype(BF16)
            for g in grad_gate_up
        ]
    )
    grad_normed_two = lax.psum_scatter(
        lax.dot_general(grad_gate_up[0], gu_full[0], nt, preferred_element_type=F32)
        + lax.dot_general(grad_gate_up[1], gu_full[1], nt, preferred_element_type=F32),
        plane,
        scatter_dimension=0,
        tiled=True,
    )
    middle_part, gain_two, bias_two = norm_backward(
        grad_normed_two, unit_two, factor_two, gains32[1]
    )
    grad_middle = out_grad.astype(F32) + middle_part
    branch = lax.all_gather(grad_middle.astype(BF16), plane, axis=0, tiled=True)
    grad_mixed = lax.dot_general(branch, out_full, nt, preferred_element_type=F32)
    grad_mixed = grad_mixed.astype(BF16).reshape(shape4)
    out_weight_grad = lax.dot_general(mixed_flat, branch, tn, preferred_element_type=F32)
    scores = masked_scores(q, kk, segments)
    probs32 = jnp.exp(scores - log_totals)
    dp = jnp.einsum("gbhe,gshe->ghbs", grad_mixed, v, preferred_element_type=F32)
    inner = jnp.sum(probs32 * dp, axis=-1, keepdims=True)
    grad_scores = (probs32 * (dp - inner)).astype(BF16)
    factor = 1.0 / math.sqrt(HEAD)
    gq = jnp.einsum("ghbs,gshe->gbhe", grad_scores, kk, preferred_element_type=F32) * factor
    gk = jnp.einsum("ghbs,gbhe->gshe", grad_scores, q, preferred_element_type=F32) * factor
    gv = jnp.einsum(
        "ghbs,gbhe->gshe", probs32.astype(BF16), grad_mixed, preferred_element_type=F32
    )
    flat = (tokens, heads, HEAD)
    gp = [
        unrotate(gq.reshape(flat), cos, sin),
        unrotate(gk.reshape(flat), cos, sin),
        gv.reshape(flat),
    ]
    gp = [g.reshape(tokens, qc).astype(BF16) for g in gp]
    qkv_grad = jnp.stack(
        [lax.dot_general(normed_full, g, tn, preferred_element_type=F32).astype(BF16) for g in gp]
    )
    sums = jnp.stack([jnp.sum(gp[c].astype(F32), axis=0) for c in (0, 2)])
    grad_normed = sum(
        lax.dot_general(gp[c], qkv_full[c], nt, preferred_element_type=F32) for c in range(3)
    )
    grad_normed = lax.psum_scatter(grad_normed, plane, scatter_dimension=0, tiled=True)
    stream_part, gain_one, bias_one = norm_backward(grad_normed, unit_one, factor_one, gains32[0])
    input_grad = (grad_middle + stream_part).astype(BF16)

    parts = line_call(
        False,
        lines,
        [qkv_grad, out_weight_grad.astype(BF16), gate_up_grad, down_grad.astype(BF16)],
    )
    dq, do, dg, dd = (jnp.sum(p.astype(F32), axis=0) for p in parts)

    def finish(total, axis, column_axis):
        shape = total.shape
        halves = total.reshape(shape[:axis] + (2, shape[axis] // 2) + shape[axis + 1 :])
        own, came = exchange_y(jnp.moveaxis(halves, axis, 0), y)
        return swap_y(own, came, y, column_axis)

    qkv_out = finish(dq, 1, 2)
    out_out = finish(do, 1, 0)
    gu_out = finish(dg, 1, 2)
    down_out = finish(dd, 1, 0)
    vectors = jnp.stack([gain_one, gain_two, bias_one, bias_two])
    vectors = lax.psum(vectors, "tp")
    vectors = lax.psum_scatter(vectors, ("z", "y"), scatter_dimension=1, tiled=True)
    both = lax.dynamic_update_slice_in_dim(
        jnp.zeros((2, 2 * heads, HEAD), F32), sums.reshape(2, heads, HEAD), y * heads, 1
    )
    bias_out = lax.psum_scatter(both, ("z", "y"), scatter_dimension=2, tiled=True)
    return (
        layer_out,
        input_grad,
        qkv_out,
        bias_out,
        out_out,
        gu_out,
        down_out,
        vectors[:2],
        vectors[2:],
    )


def solution(mesh):
    groups, tp = mesh.shape["fsdp"], mesh.shape["tp"]
    lines = groups // 2
    cube = Mesh(mesh.devices.reshape(lines, 2, tp), ("z", "y", "tp"))
    fsdp = ("z", "y")
    token = P(("z", "y", "tp"), None)
    placed = (
        token,
        P(fsdp, None),
        P(None, fsdp, "tp"),
        P(None, "tp", fsdp),
        P("tp", fsdp),
        P(None, fsdp, "tp"),
        P("tp", fsdp),
        P(None, fsdp),
        P(None, fsdp),
        token,
    )
    return jax.shard_map(
        functools.partial(shards, lines),
        mesh=cube,
        in_specs=placed,
        out_specs=(
            token,
            token,
            P(None, fsdp, "tp"),
            P(None, "tp", fsdp),
            P("tp", fsdp),
            P(None, fsdp, "tp"),
            P("tp", fsdp),
            P(None, fsdp),
            P(None, fsdp),
        ),
        check_vma=False,
    )
```

```python
import functools
import math

import jax
import jax.numpy as jnp
from jax import lax
from jax.experimental import pallas as pl
from jax.experimental.pallas import tpu as pltpu
from jax.sharding import Mesh
from jax.sharding import PartitionSpec as P

HEAD = 64
ROT = 16
EPSILON = 1e-05
MASKED = -1e30
ROPE_BASE = 10000.0
F32 = jnp.float32
BF16 = jnp.bfloat16
MESH = pl.DeviceIdType.MESH
LSE = 100
NN = (((1,), (0,)), ((), ()))
NT = (((1,), (1,)), ((), ()))
TN = (((0,), (0,)), ((), ()))
SCALE = 1.0 / math.sqrt(HEAD)


def dot(a, b, dims=NN):
    return lax.dot_general(a, b, dims, preferred_element_type=F32)


def tables(segments):
    length = segments.shape[0]
    positions = jnp.arange(length, dtype=jnp.int32)
    starts_here = jnp.concatenate([jnp.ones((1,), jnp.bool_), segments[1:] != segments[:-1]])
    begins = lax.cummax(jnp.where(starts_here, positions, 0), axis=0)
    offsets = (positions - begins).astype(F32)
    half_rot = ROT // 2
    frequency = ROPE_BASE ** (-(jnp.arange(half_rot, dtype=F32) * 2.0 / ROT))
    angles = offsets[:, None] * frequency[None, :]
    cos, sin = jnp.cos(angles), jnp.sin(angles)
    seg = segments.astype(F32)
    return jnp.concatenate(
        [
            cos,
            cos,
            jnp.ones((length, HEAD - ROT), F32),
            -sin,
            sin,
            jnp.zeros((length, 32 - ROT), F32),
            seg[:, None],
            jnp.zeros((length, 31), F32),
        ],
        axis=1,
    )


class Layer:
    def __init__(self, sizes, refs):
        self.__dict__.update(sizes)
        self.__dict__.update(refs)
        self.z, self.y, self.t = (lax.axis_index(a) for a in ("z", "y", "tp"))
        self.core = lax.rem(self.t, 2)
        self.x = lax.div(self.t, 2)
        self.sib = (self.z, self.y, self.t + 1 - 2 * self.core)
        self.xn = (self.z, self.y, lax.rem(self.t + 2, 4))
        self.yn = (self.z, 1 - self.y, self.t)
        self.sends = []

    def remote(self, src, dst, ssem, rsem, to):
        return pltpu.make_async_remote_copy(
            src_ref=src, dst_ref=dst, send_sem=ssem, recv_sem=rsem, device_id=to, device_id_type=MESH
        )

    def send(self, src, dst, ssem, rsem, to):
        copy = self.remote(src, dst, ssem, rsem, to)
        copy.start()
        self.sends.append(copy)

    def arrived(self, dst, rsem):
        self.remote(dst, dst, rsem, rsem, self.sib).wait_recv()

    def flush(self):
        for copy in self.sends:
            copy.wait_send()
        self.sends = []

    def chip_rows(self, y, x):
        return pl.multiple_of((y * 2 + x) * 2 * self.own, 2 * self.own)

    def chips(self):
        y, x = self.y, self.x
        return [
            self.chip_rows(1 - y, 1 - x),
            self.chip_rows(1 - y, x),
            self.chip_rows(y, 1 - x),
            self.chip_rows(y, x),
        ]

    def gather_start(self, u, buf):
        own, c = self.own, self.core
        mine = buf.at[pl.ds(pl.multiple_of(self.chips()[3] + c * own, own), own)]
        ss, rs = self.ag_send, self.ag_recv
        self.send(mine, mine, ss.at[u, 0], rs.at[u, 0], self.sib)
        self.send(mine, mine, ss.at[u, 1], rs.at[u, 1], self.xn)
        self.send(mine, mine, ss.at[u, 2], rs.at[u, 2], self.yn)

    def gather_relay(self, u, buf):
        own, c = self.own, self.core
        half = own // 2
        d, yr, xr, s = self.chips()
        ss, rs = self.ag_send, self.ag_recv

        def part(base, off, n):
            return buf.at[pl.ds(pl.multiple_of(base + c * own + off, half), n)]

        bx, by = part(xr, 0, own), part(yr, 0, own)
        self.arrived(bx, rs.at[u, 1])
        self.send(part(xr, 0, half), part(xr, 0, half), ss.at[u, 3], rs.at[u, 3], self.yn)
        self.send(bx, bx, ss.at[u, 4], rs.at[u, 4], self.sib)
        self.arrived(by, rs.at[u, 2])
        self.send(part(yr, half, half), part(yr, half, half), ss.at[u, 5], rs.at[u, 5], self.xn)
        self.send(by, by, ss.at[u, 6], rs.at[u, 6], self.sib)

    def gather_last(self, u, buf):
        own, c = self.own, self.core
        half = own // 2
        d = self.chips()[0]
        ss, rs = self.ag_send, self.ag_recv

        def part(off):
            return buf.at[pl.ds(pl.multiple_of(d + c * own + off, half), half)]

        self.arrived(part(0), rs.at[u, 3])
        self.send(part(0), part(0), ss.at[u, 7], rs.at[u, 7], self.sib)
        self.arrived(part(half), rs.at[u, 5])
        self.send(part(half), part(half), ss.at[u, 8], rs.at[u, 8], self.sib)

    def gather_wait(self, u, buf):
        own, c = self.own, self.core
        half = own // 2
        d, yr, xr, s = self.chips()
        rs = self.ag_recv

        def part(base, off, n):
            return buf.at[pl.ds(pl.multiple_of(base + (1 - c) * own + off, half), n)]

        self.arrived(part(s, 0, own), rs.at[u, 0])
        self.arrived(part(xr, 0, own), rs.at[u, 4])
        self.arrived(part(yr, 0, own), rs.at[u, 6])
        self.arrived(part(d, 0, half), rs.at[u, 7])
        self.arrived(part(d, half, half), rs.at[u, 8])

    def reduce_start(self, u, compute):
        own, c = self.own, self.core
        if u > 0:
            pl.semaphore_wait(self.free, 3)
            for copy in self.rs_sends:
                copy.wait_send()
        self.rs_sends = []
        self.core_sends = []
        for j, row in enumerate(self.chips()):
            compute(j, row)
            there = pl.ds(pl.multiple_of(j * 2 * own + (1 - c) * own, own), own)
            self.csend[j] = self.fbig[there, :].astype(BF16)
            copy = self.remote(
                self.csend.at[j], self.crecv.at[j], self.rs_send.at[u, j], self.rs_recv.at[u, j], self.sib
            )
            copy.start()
            self.core_sends.append(copy)

    def reduce_send(self, *what):
        copy = self.remote(*what)
        copy.start()
        self.rs_sends.append(copy)

    def reduce_mine(self, j, at=0, rows=None):
        own, c = self.own, self.core
        rows = own if rows is None else rows
        return self.fbig[pl.ds(pl.multiple_of(j * 2 * own + c * own + at, rows), rows), :]

    def reduce_diagonal(self, u):
        half = self.own // 2
        ss, rs = self.rs_send, self.rs_recv
        self.arrived(self.crecv.at[0], rs.at[u, 0])
        self.core_sends[0].wait_send()
        self.csend[0] = (self.reduce_mine(0) + self.crecv[0].astype(F32)).astype(BF16)
        first, second = pl.ds(0, half), pl.ds(half, half)
        self.reduce_send(self.csend.at[0, first], self.dvia.at[0], ss.at[u, 4], rs.at[u, 4], self.xn)
        self.reduce_send(self.csend.at[0, second], self.dvia.at[1], ss.at[u, 5], rs.at[u, 5], self.yn)

    def reduce_straight(self, u):
        own, half = self.own, self.own // 2
        ss, rs = self.rs_send, self.rs_recv
        for j, mixes, to in ((1, 0, self.yn), (2, 1, self.xn)):
            self.arrived(self.crecv.at[j], rs.at[u, j])
            self.core_sends[j].wait_send()
            for h in (1 - mixes, mixes):
                total = self.reduce_mine(j, h * half, half) + self.crecv[j, h * half : (h + 1) * half].astype(F32)
                if h == mixes:
                    self.arrived(self.dvia.at[j - 1], rs.at[u, 3 + j])
                    total = total + self.dvia[j - 1].astype(F32)
                self.csend[j, h * half : (h + 1) * half] = total.astype(BF16)
            self.reduce_send(self.csend.at[j], self.hrecv.at[j - 1], ss.at[u, 5 + j], rs.at[u, 5 + j], to)

    def reduce_finish(self, u, body):
        rs = self.rs_recv
        self.arrived(self.crecv.at[3], rs.at[u, 3])
        self.arrived(self.hrecv.at[0], rs.at[u, 6])
        self.arrived(self.hrecv.at[1], rs.at[u, 7])
        tile = 32

        @pl.loop(0, self.own // tile)
        def _(n):
            at = pl.multiple_of(n * tile, tile)
            rows = pl.ds(at, tile)
            total = self.reduce_mine(3, at, tile) + self.crecv[3, rows, :].astype(F32)
            total = total + self.hrecv[0, rows, :].astype(F32) + self.hrecv[1, rows, :].astype(F32)
            body(rows, total)

        self.core_sends[3].wait_send()
        if u < 3:
            for to in (self.sib, self.xn, self.yn):
                pl.semaphore_signal(self.free, inc=1, device_id=to, device_id_type=MESH)

    def item(self, m, zz):
        rows = pl.ds(pl.multiple_of(zz * self.depth, self.depth), self.depth)
        if m == 0:
            return self.wq.at[:, rows]
        if m == 1:
            return self.wo.at[zz]
        if m in (2, 3):
            return self.wg.at[m - 2, rows]
        return self.wd.at[zz]

    def line_start(self, m):
        z, n = self.z, self.lines
        for step in range(1, n):
            to = lax.rem(z + step, n)

            def go(to=to, step=step):
                self.remote(
                    self.item(m, z),
                    self.item(m, z),
                    self.z_send.at[m, step],
                    self.z_recv.at[m, z],
                    (to, self.y, self.t),
                ).start()

            if n == 4 and step in (1, 3):
                pl.when(self.straight(step))(go)
            else:
                go()

    def straight(self, step):
        return jnp.logical_not((self.z == 3) if step == 1 else (self.z == 0))

    def line_flush(self, m):
        z, n = self.z, self.lines
        for step in range(1, n):

            def done(step=step):
                self.remote(
                    self.item(m, z),
                    self.item(m, z),
                    self.z_send.at[m, step],
                    self.z_recv.at[m, z],
                    (z, self.y, self.t),
                ).wait_send()

            if n == 4 and step in (1, 3):
                pl.when(self.straight(step))(done)
            else:
                done()
        if n == 4:

            @pl.when((z == 1) | (z == 2))
            def _():
                far = jnp.where(z == 1, 3, 0)
                self.remote(
                    self.item(m, far),
                    self.item(m, far),
                    self.z_send.at[m, 0],
                    self.z_recv.at[m, far],
                    (z, self.y, self.t),
                ).wait_send()

    def line_order(self, s):
        z, n = self.z, self.lines
        if n != 4:
            return lax.rem(z + s, n)
        low = z < 2
        if s == 0:
            return z
        if s == 1:
            return z + 1 - 2 * lax.rem(z, 2)
        if s == 2:
            return jnp.where(low, 2, 1)
        return jnp.where(low, 3, 0)

    def line_wait(self, m, s):
        zz = self.line_order(s)
        if s == 0:
            return zz
        self.arrived(self.item(m, zz), self.z_recv.at[m, zz])
        if self.lines == 4 and s == 3:
            z = self.z

            @pl.when((z == 1) | (z == 2))
            def _():
                self.remote(
                    self.item(m, zz),
                    self.item(m, zz),
                    self.z_send.at[m, 0],
                    self.z_recv.at[m, zz],
                    (3 * (z - 1), self.y, self.t),
                ).start()

        return zz

    def is_end(self):
        return (self.z == 0) | (self.z == 3)

    def relayed(self, m):
        return self.lines == 4 and m in (0, 2, 3)

    def part(self, m, zz):
        return self.gd.at[zz] if m == 4 else self.item(m, zz)

    def relay(self, m):
        return self.relay_q if m == 0 else self.relay_g.at[m - 2]

    def landing(self, m):
        return (self.r_q, self.r_o, self.r_g, self.r_u, self.r_d)[m]

    def part_order(self, i):
        n = self.lines
        if i == n - 1:
            return self.z
        if n != 4:
            return self.line_order(i + 1)
        if i == 1:
            return self.line_order(2)
        first, last = (3, 1) if i == 0 else (1, 3)
        return jnp.where(self.is_end(), self.line_order(first), self.line_order(last))

    def part_send(self, m, i):
        z, n = self.z, self.lines
        zz = self.part_order(i)

        def straight():
            self.remote(
                self.part(m, zz),
                self.landing(m).at[z],
                self.g_send.at[m, i],
                self.g_recv.at[m, z],
                (zz, self.y, self.t),
            ).start()

        if not self.relayed(m):
            straight()
            return
        if i == 0:

            @pl.when(self.is_end())
            def _():
                self.remote(
                    self.part(m, zz),
                    self.relay(m),
                    self.g_send.at[m, 0],
                    self.g_relay.at[m],
                    (jnp.where(z == 0, 1, 2), self.y, self.t),
                ).start()

            pl.when(jnp.logical_not(self.is_end()))(straight)
            return
        if i == 2:

            @pl.when(jnp.logical_not(self.is_end()))
            def _():
                self.arrived(self.relay(m), self.g_relay.at[m])
                mine, came = self.part(m, zz), self.relay(m)
                mine[...] = (mine[...].astype(F32) + came[...].astype(F32)).astype(BF16)

        straight()

    def part_flush(self, m):
        for i in range(self.lines - 1):
            self.remote(
                self.part(m, self.z),
                self.landing(m).at[self.z],
                self.g_send.at[m, i],
                self.g_recv.at[m, self.z],
                self.sib,
            ).wait_send()

    def place(self, m, p):
        fit = self.tokens // self.depth
        if m in (1, 4):
            return pl.ds(0, self.qc if m == 1 else self.fc), pl.ds(p * self.depth, self.depth)
        rows = pl.ds((p % fit) * self.depth, self.depth)
        width = self.qc if m == 0 else self.fpad
        return rows, pl.ds((p // fit) * max(3 * self.qc, self.fpad), width)

    def part_land(self, m):
        copies = []
        for p in range(self.lines - 1):
            slot = self.line_order(p + 1)
            rows, lanes = self.place(m, p)

            def fetch(act, p=p, slot=slot, rows=rows, lanes=lanes):
                src = self.landing(m).at[slot]
                if m == 0:
                    for j in range(3):
                        at = pl.ds(lanes.start + j * self.qc, self.qc)
                        copy = pltpu.make_async_copy(
                            src.at[j], self.h2.at[rows, at], self.g_load.at[p, j]
                        )
                        getattr(copy, act)()
                else:
                    copy = pltpu.make_async_copy(src, self.h2.at[rows, lanes], self.g_load.at[p, 0])
                    getattr(copy, act)()

            def begin(fetch=fetch, slot=slot):
                self.arrived(self.landing(m).at[slot], self.g_recv.at[m, slot])
                fetch("start")

            if self.relayed(m) and p == 2:
                pl.when(jnp.logical_not(self.is_end()))(begin)

                @pl.when(self.is_end())
                def _():
                    if m == 0:
                        lanes_all = pl.ds(lanes.start, 3 * self.qc)
                    else:
                        lanes_all = lanes
                    self.h2[rows, lanes_all] = jnp.zeros((rows.size, lanes_all.size), BF16)

                copies.append((fetch, True))
            else:
                begin()
                copies.append((fetch, False))
        for fetch, middle_only in copies:
            if middle_only:
                pl.when(jnp.logical_not(self.is_end()))(functools.partial(fetch, "wait"))
            else:
                fetch("wait")

    def enter(self):
        z, y, t = self.z, self.y, self.t
        barrier = pltpu.get_barrier_semaphore()
        n = 2 * self.lines
        f = z * 2 + y
        others = []
        for step in range(1, n):
            g = lax.rem(f + step, n)
            others.append((lax.div(g, 2), lax.rem(g, 2), t))
        for to in others + [self.sib, self.xn]:
            pl.semaphore_signal(barrier, inc=1, device_id=to, device_id_type=MESH)
        pl.semaphore_wait(barrier, n + 1)
        return f, others

    def unit_rows(self, rows):
        mean = jnp.mean(rows, axis=-1, keepdims=True)
        centred = rows - mean
        factor = lax.rsqrt(jnp.mean(centred * centred, axis=-1, keepdims=True) + EPSILON)
        return centred * factor, factor

    def rope_tables(self, g):
        rows = pl.ds(pl.multiple_of(g * self.length, self.length), self.length)
        both = self.tab[rows, :]
        lane = lax.broadcasted_iota(jnp.int32, both.shape, 1)
        turned = pltpu.roll(both, 64, 1)
        cos = jnp.where(lane < 64, both, turned)
        sin = jnp.where(lane < 64, turned, both)
        dim = lax.rem(lane, HEAD)
        seg = self.tab[rows, 96:97]
        return cos, jnp.where(dim < ROT, sin, 0.0), dim, seg

    def turn(self, v, dim):
        ahead = pltpu.roll(v, 128 - ROT // 2, 1)
        behind = pltpu.roll(v, ROT // 2, 1)
        return jnp.where(dim < ROT // 2, ahead, jnp.where(dim < ROT, behind, 0.0))

    def masked(self, scores, seg, g, r0):
        rows, cols = scores.shape
        at = lax.broadcasted_iota(jnp.int32, scores.shape, 0) + r0
        key = lax.broadcasted_iota(jnp.int32, scores.shape, 1)
        seg_row = self.segrow[g, 0:1, 0:cols]
        return jnp.where((seg == seg_row) & (at >= key), scores * SCALE, MASKED)


def forward(k):
    own, length, tokens = k.own, k.length, 2 * k.length
    width, rows_f, depth = k.width, k.rows, k.depth
    c, y = k.core, k.y
    f, others = k.enter()
    loads = k.loads
    for i, (src, dst) in enumerate(
        (
            (k.in_gu.at[0], k.og.at[pl.ds(0, rows_f), pl.ds(0, 2 * k.fc)]),
            (k.in_gu.at[1], k.og.at[pl.ds(rows_f, rows_f), pl.ds(0, 2 * k.fc)]),
            (k.in_qkv.at[:, :, pl.ds(pl.multiple_of(y * k.qc, k.qc), k.qc)],
             k.wq.at[:, pl.ds(pl.multiple_of(f * rows_f, rows_f), rows_f)]),
            (k.in_out.at[pl.ds(pl.multiple_of(y * k.qc, k.qc), k.qc)], k.sout.at[y]),
            (k.in_down.at[pl.ds(pl.multiple_of(y * k.fc, 16), k.fc)], k.sdown.at[y]),
        )
    ):
        pltpu.make_async_copy(src, dst, loads.at[i]).start()
    k.small[f] = k.in_small[...]
    for i, to in enumerate(others):
        k.send(k.in_small, k.small.at[f], k.sm_send.at[i], k.sm_recv.at[f], to)
    mine = pl.ds(pl.multiple_of(y * length, length), length)
    k.tab[mine, :] = k.in_tab[...]
    k.segrow[y] = k.in_seg[...]
    k.send(k.in_tab, k.tab.at[mine], k.yx_send.at[0], k.yx_recv.at[0], k.yn)
    k.send(k.in_seg, k.segrow.at[y], k.yx_send.at[1], k.yx_recv.at[1], k.yn)
    away = 1 - y
    frows = pl.ds(pl.multiple_of(f * rows_f, rows_f), rows_f)
    k.send(
        k.in_qkv.at[:, :, pl.ds(pl.multiple_of(away * k.qc, k.qc), k.qc)],
        k.wq.at[:, frows],
        k.yx_send.at[2], k.yx_recv.at[2], k.yn,
    )
    k.send(
        k.in_out.at[pl.ds(pl.multiple_of(away * k.qc, k.qc), k.qc)],
        k.sout.at[y],
        k.yx_send.at[3], k.yx_recv.at[3], k.yn,
    )
    unit, _ = k.unit_rows(k.in_res[...].astype(F32))
    for i in range(2):
        raw = pl.ds(i * rows_f, rows_f)
        pltpu.make_async_copy(k.in_gu.at[i], k.og.at[raw, pl.ds(0, 2 * k.fc)], loads.at[i]).wait()
        low, high = k.og[raw, 0 : k.fc], k.og[raw, k.fc : 2 * k.fc]
        k.wg[i, frows, 0 : k.fc] = jnp.where(y == 0, low, high)
        k.gu_away[i, :, 0 : k.fc] = jnp.where(y == 0, high, low)
        k.send(
            k.gu_away.at[i], k.wg.at[i, frows], k.yx_send.at[4 + i], k.yx_recv.at[4 + i], k.yn
        )
    k.send(
        k.in_down.at[pl.ds(pl.multiple_of(away * k.fc, 16), k.fc)],
        k.sdown.at[y],
        k.yx_send.at[6], k.yx_recv.at[6], k.yn,
    )
    for step in range(1, len(others) + 1):
        g = lax.rem(f + step, len(others) + 1)
        k.arrived(k.small.at[g], k.sm_recv.at[g])
    for g in range(len(others) + 1):
        k.gains[:, g * rows_f : (g + 1) * rows_f] = k.small[g, 0:4, 0:rows_f]
    bias = k.small[0, 4:6, :]
    for g in range(1, len(others) + 1):
        bias = bias + k.small[g, 4:6, :]
    bias = jnp.where(y == 0, bias[:, 0 : k.qc], bias[:, k.qc : 2 * k.qc])
    at = k.chips()[3] + c * own
    mine_rows = pl.ds(pl.multiple_of(at, own), own)
    k.h1[mine_rows, :] = (unit * k.gains[0:1, :] + k.gains[2:3, :]).astype(BF16)
    k.gather_start(0, k.h1)

    pltpu.make_async_copy(k.in_qkv.at[:, :, pl.ds(0, k.qc)], k.wq.at[:, frows], loads.at[2]).wait()
    nrows = pl.ds(pl.multiple_of((f + 1 - 2 * y) * rows_f, rows_f), rows_f)
    k.arrived(k.wq.at[:, nrows], k.yx_recv.at[2])
    k.line_start(0)
    pltpu.make_async_copy(k.in_out.at[pl.ds(0, k.qc)], k.sout.at[0], loads.at[3]).wait()
    k.arrived(k.sout.at[away], k.yx_recv.at[3])
    k.wo[k.z] = jnp.concatenate([k.sout[0], k.sout[1]], axis=1)
    k.line_start(1)
    k.gather_relay(0, k.h1)
    for i in range(2):
        k.arrived(k.wg.at[i, nrows], k.yx_recv.at[4 + i])
        k.line_start(2 + i)
    pltpu.make_async_copy(k.in_down.at[pl.ds(0, k.fc)], k.sdown.at[0], loads.at[4]).wait()
    k.arrived(k.sdown.at[away], k.yx_recv.at[6])
    k.wd[k.z] = jnp.concatenate([k.sdown[0], k.sdown[1]], axis=1)
    k.line_start(4)
    k.gather_last(0, k.h1)
    k.arrived(k.tab.at[pl.ds(pl.multiple_of(away * length, length), length)], k.yx_recv.at[0])
    k.arrived(k.segrow.at[away], k.yx_recv.at[1])
    k.gather_wait(0, k.h1)
    k.og[mine_rows, :] = k.in_og[...]
    k.gather_start(1, k.og)

    tile = 256
    for s in range(k.lines):
        zz = k.line_wait(0, s)
        cols = pl.ds(pl.multiple_of(zz * depth, depth), depth)

        @pl.loop(0, tokens // tile)
        def _(i):
            rows = pl.ds(pl.multiple_of(i * tile, tile), tile)
            a = k.h1[rows, cols]
            for j in range(3):
                out = dot(a, k.wq[j, cols, :])
                into = pl.ds(j * k.qc, k.qc)
                if s == 0:
                    k.fbig[rows, into] = out
                else:
                    k.fbig[rows, into] += out

    k.gather_relay(1, k.og)

    pairs = k.qc // 128
    block = 256

    @pl.loop(0, 2)
    def _(g):
        rows = pl.ds(pl.multiple_of(g * length, length), length)
        cos, sin, dim, seg = k.rope_tables(g)
        for p in range(pairs):
            into = pl.ds(p * 128, 128)

            def part(j):
                return k.fbig[rows, pl.ds(j * k.qc + p * 128, 128)]

            q = part(0) + bias[0:1, p * 128 : (p + 1) * 128]
            kk = part(1)
            k.qkv[0, rows, into] = (q * cos + k.turn(q, dim) * sin).astype(BF16)
            k.qkv[1, rows, into] = (kk * cos + k.turn(kk, dim) * sin).astype(BF16)
            k.qkv[2, rows, into] = (part(2) + bias[1:2, p * 128 : (p + 1) * 128]).astype(BF16)
            for r in range(0, length, block):
                some = pl.ds(pl.multiple_of(g * length + r, block), block)
                seen = pl.ds(pl.multiple_of(g * length, length), r + block)
                qb = k.qkv[0, some, into]
                kb = k.qkv[1, seen, into]
                vb = k.qkv[2, seen, into]
                low = lax.broadcasted_iota(jnp.int32, (block, 128), 1) < HEAD
                both = []
                marks = []
                for h in range(2):
                    mask = low if h == 0 else jnp.logical_not(low)
                    scores = dot(jnp.where(mask, qb, jnp.zeros_like(qb)), kb, NT)
                    scores = k.masked(scores, seg[r : r + block], g, r)
                    top = jnp.max(scores, axis=-1, keepdims=True)
                    e = jnp.exp(scores - top)
                    total = jnp.sum(e, axis=-1, keepdims=True)
                    probs = (e / total).astype(BF16)
                    both.append(dot(probs, vb))
                    marks.append(top + jnp.log(total))
                k.mixed[some, into] = jnp.where(low, both[0], both[1]).astype(BF16)
                at_lane = lax.broadcasted_iota(jnp.int32, (block, 128), 1)
                old = k.tab[some, :]
                old = jnp.where(at_lane == LSE + 2 * p, marks[0], old)
                k.tab[some, :] = jnp.where(at_lane == LSE + 2 * p + 1, marks[1], old)

    k.gather_last(1, k.og)
    for s in range(k.lines):
        k.line_wait(1, s)

    def project(j, row):
        a = k.mixed[pl.ds(row, 2 * own), :]
        for zz in range(k.lines):
            k.fbig[j * 2 * own : (j + 1) * 2 * own, zz * depth : (zz + 1) * depth] = dot(a, k.wo[zz])

    k.reduce_start(0, project)
    k.reduce_diagonal(0)
    k.reduce_straight(0)

    def second_norm(rows, total):
        middle = k.in_res[rows, :].astype(F32) + total
        k.middle[rows, :] = middle
        unit, _ = k.unit_rows(middle)
        into = pl.ds(pl.multiple_of(at + rows.start, 32), rows.size)
        k.h2[into, :] = (unit * k.gains[1:2, :] + k.gains[3:4, :]).astype(BF16)

    k.reduce_finish(0, second_norm)
    k.gather_start(2, k.h2)
    k.gather_wait(1, k.og)
    k.gather_relay(2, k.h2)
    k.gather_last(2, k.h2)
    k.gather_wait(2, k.h2)

    for i in range(2):
        for s in range(k.lines):
            zz = k.line_wait(2 + i, s)
            cols = pl.ds(pl.multiple_of(zz * depth, depth), depth)

            @pl.loop(0, tokens // tile)
            def _(n):
                rows = pl.ds(pl.multiple_of(n * tile, tile), tile)
                out = dot(k.h2[rows, cols], k.wg[i, cols, 0 : k.fc])
                into = pl.ds(i * k.fpad, k.fc)
                if s == 0:
                    k.fbig[rows, into] = out
                else:
                    k.fbig[rows, into] += out

    @pl.loop(0, tokens // 64)
    def _(n):
        rows = pl.ds(pl.multiple_of(n * 64, 64), 64)
        gate = k.fbig[rows, 0 : k.fc]
        up = k.fbig[rows, k.fpad : k.fpad + k.fc]
        sig = 1.0 / (1.0 + jnp.exp(-gate))
        silu = gate * sig
        k.hidden[rows, :] = (silu * up).astype(BF16)
        k.by_gate[rows, :] = (up * sig * (1.0 + gate * (1.0 - sig))).astype(BF16)
        k.by_up[rows, :] = silu.astype(BF16)


def norm_back(k, which, grad, unit, factor):
    k.vecs[which : which + 1, :] += jnp.sum(grad * unit, axis=0, keepdims=True)
    k.vecs[which + 2 : which + 3, :] += jnp.sum(grad, axis=0, keepdims=True)
    scaled = grad * k.gains[which : which + 1, :]
    centred = scaled - jnp.mean(scaled, axis=-1, keepdims=True)
    return factor * (centred - unit * jnp.mean(scaled * unit, axis=-1, keepdims=True))


def weight_grads(k, m, block):
    for i in range(k.lines):
        block(k.part_order(i))
        if i < k.lines - 1:
            k.part_send(m, i)


def backward(k):
    own, length, tokens = k.own, k.length, k.tokens
    depth, fc, qc = k.depth, k.fc, k.qc
    c, y, z = k.core, k.y, k.z
    tile = 256
    at_own = k.chips()[3] + c * own
    k.vecs[...] = jnp.zeros_like(k.vecs)

    def down_block(zz):
        cols = pl.ds(pl.multiple_of(zz * depth, depth), depth)
        k.gd[zz] = dot(k.hidden[...], k.og[:, cols], TN).astype(BF16)

    weight_grads(k, 4, down_block)

    for s in range(k.lines):
        zz = k.line_wait(4, s)
        cols = pl.ds(pl.multiple_of(zz * depth, depth), depth)

        @pl.loop(0, tokens // tile)
        def _(n):
            rows = pl.ds(pl.multiple_of(n * tile, tile), tile)
            out = dot(k.og[rows, cols], k.wd[zz], NT)
            if s == 0:
                k.fbig[rows, 0:fc] = out
            else:
                k.fbig[rows, 0:fc] += out

    @pl.loop(0, tokens // 64)
    def _(n):
        rows = pl.ds(pl.multiple_of(n * 64, 64), 64)
        grad = k.fbig[rows, 0:fc]
        k.by_gate[rows, :] = (grad * k.by_gate[rows, :].astype(F32)).astype(BF16)
        k.by_up[rows, :] = (grad * k.by_up[rows, :].astype(F32)).astype(BF16)

    def back_two(j, row):
        rows = pl.ds(row, 2 * own)
        gate, up = k.by_gate[rows, :], k.by_up[rows, :]
        for n in range(0, k.width, 512):
            some = pl.ds(n, 512)
            out = dot(gate, k.wg[0, some, 0:fc], NT) + dot(up, k.wg[1, some, 0:fc], NT)
            k.fbig[j * 2 * own : (j + 1) * 2 * own, n : n + 512] = out

    k.flush()
    k.reduce_start(1, back_two)
    k.reduce_diagonal(1)
    k.line_flush(2)
    k.line_flush(3)

    def gate_block(i):
        def block(zz):
            cols = pl.ds(pl.multiple_of(zz * depth, depth), depth)
            grads = k.by_gate if i == 0 else k.by_up
            k.wg[i, cols, 0:fc] = dot(k.h2[:, cols], grads[...], TN).astype(BF16)

        return block

    k.reduce_straight(1)
    weight_grads(k, 2, gate_block(0))

    def second_back(rows, total):
        unit, factor = k.unit_rows(k.middle[rows, :])
        back = norm_back(k, 1, total, unit, factor)
        grad_middle = k.in_og[rows, :].astype(F32) + back
        k.gmid[rows, :] = grad_middle
        into = pl.ds(pl.multiple_of(at_own + rows.start, 32), rows.size)
        k.og[into, :] = grad_middle.astype(BF16)

    k.reduce_finish(1, second_back)
    k.gather_start(3, k.og)
    weight_grads(k, 3, gate_block(1))
    k.gather_relay(3, k.og)
    k.gather_last(3, k.og)
    k.gather_wait(3, k.og)

    @pl.loop(0, tokens // tile)
    def _(n):
        rows = pl.ds(pl.multiple_of(n * tile, tile), tile)
        out = dot(k.og[rows, 0:depth], k.wo[0], NT)
        for zz in range(1, k.lines):
            out = out + dot(k.og[rows, zz * depth : (zz + 1) * depth], k.wo[zz], NT)
        k.h2[rows, 0:qc] = out.astype(BF16)

    block = 256
    k.bsum[...] = jnp.zeros_like(k.bsum)

    @pl.loop(0, 2)
    def _(g):
        rows = pl.ds(pl.multiple_of(g * length, length), length)
        cos, sin, dim, seg = k.rope_tables(g)
        for p in range(qc // 128):
            into = pl.ds(p * 128, 128)
            for r in range(0, length, block):
                some = pl.ds(pl.multiple_of(g * length + r, block), block)
                seen = pl.ds(pl.multiple_of(g * length, length), r + block)
                qb = k.qkv[0, some, into]
                kb = k.qkv[1, seen, into]
                vb = k.qkv[2, seen, into]
                gb = k.h2[some, into]
                lane = lax.broadcasted_iota(jnp.int32, (block, 128), 1)
                low = lane < HEAD
                marks = k.tab[some, :]
                gq, gk, gv = [], [], []
                for h in range(2):
                    mask = low if h == 0 else jnp.logical_not(low)
                    qm = jnp.where(mask, qb, jnp.zeros_like(qb))
                    gm = jnp.where(mask, gb, jnp.zeros_like(gb))
                    mark = jnp.sum(jnp.where(lane == LSE + 2 * p + h, marks, 0.0), axis=1, keepdims=True)
                    scores = k.masked(dot(qm, kb, NT), seg[r : r + block], g, r)
                    probs = jnp.exp(scores - mark)
                    dp = dot(gm, vb, NT)
                    inner = jnp.sum(probs * dp, axis=-1, keepdims=True)
                    gs = (probs * (dp - inner)).astype(BF16)
                    gq.append(dot(gs, kb))
                    gk.append(dot(gs, qm, TN))
                    gv.append(dot(probs.astype(BF16), gm, TN))
                k.fbig[some, pl.ds(p * 128, 128)] = jnp.where(low, gq[0], gq[1]) * SCALE
                for j, v in ((1, (gk[0] + gk[1]) * SCALE), (2, gv[0] + gv[1])):
                    cols = pl.ds(j * qc + p * 128, 128)
                    if r > 0:
                        before = pl.ds(pl.multiple_of(g * length, length), r)
                        k.fbig[before, cols] += v[0:r]
                    k.fbig[some, cols] = v[r : r + block]
            for j in range(3):
                v = k.fbig[rows, pl.ds(j * qc + p * 128, 128)]
                if j < 2:
                    v = v * cos + k.turn(v * sin, dim)
                v = v.astype(BF16)
                k.qkv[j, rows, into] = v
                if j != 1:
                    half = j // 2
                    k.bsum[half : half + 1, into] += jnp.sum(v.astype(F32), axis=0, keepdims=True)

    def back_one(j, row):
        rows = pl.ds(row, 2 * own)
        parts = [k.qkv[i, rows, :] for i in range(3)]
        for n in range(0, k.width, 512):
            some = pl.ds(n, 512)
            out = dot(parts[0], k.wq[0, some, :], NT)
            for i in (1, 2):
                out = out + dot(parts[i], k.wq[i, some, :], NT)
            k.fbig[j * 2 * own : (j + 1) * 2 * own, n : n + 512] = out

    k.reduce_start(2, back_one)
    k.line_flush(0)
    k.line_flush(1)
    k.reduce_diagonal(2)

    def qkv_block(zz):
        cols = pl.ds(pl.multiple_of(zz * depth, depth), depth)
        for i in range(3):
            k.wq[i, cols, :] = dot(k.h1[:, cols], k.qkv[i], TN).astype(BF16)

    def out_block(zz):
        cols = pl.ds(pl.multiple_of(zz * depth, depth), depth)
        k.wo[zz] = dot(k.mixed[...], k.og[:, cols], TN).astype(BF16)

    weight_grads(k, 1, out_block)
    k.reduce_straight(2)
    weight_grads(k, 0, qkv_block)

    def first_back(rows, total):
        unit, factor = k.unit_rows(k.in_res[rows, :].astype(F32))
        back = norm_back(k, 0, total, unit, factor)
        k.o_input[rows, :] = (k.gmid[rows, :] + back).astype(BF16)

    k.reduce_finish(2, first_back)


def vectors(k):
    f = k.z * 2 + k.y
    n = 2 * k.lines
    rows = k.rows
    k.vsend[...] = jnp.zeros_like(k.vsend)
    for g in range(n):
        k.vsend[g, 0:4, 0:rows] = k.vecs[0:4, g * rows : (g + 1) * rows]
        k.vsend[g, 4:6, 0 : k.qc] = k.bsum[0:2, :]
    for step in range(1, n):
        g = lax.rem(f + step, n)
        k.send(
            k.vsend.at[g], k.vrecv.at[f], k.v_send.at[step], k.v_recv.at[f],
            (lax.div(g, 2), lax.rem(g, 2), k.t),
        )
    k.vrecv[f] = k.vsend[f]
    for step in range(1, n):
        g = lax.rem(f + step, n)
        k.arrived(k.vrecv.at[g], k.v_recv.at[g])
    total = k.vrecv[0]
    sides = [k.vrecv[0], k.vrecv[1]]
    for g in range(1, n):
        total = total + k.vrecv[g]
        if g > 1:
            sides[g % 2] = sides[g % 2] + k.vrecv[g]
    k.o_bias[:, 0 : k.qc] = sides[0][:, 0 : k.qc]
    k.o_bias[:, k.qc : 2 * k.qc] = sides[1][:, 0 : k.qc]
    k.tsum[0] = total
    k.send(k.tsum.at[0], k.trecv.at[0], k.t_send.at[0], k.t_recv.at[0], k.sib)
    k.arrived(k.trecv.at[0], k.t_recv.at[0])
    k.tsum[1] = total + k.trecv[0]
    k.send(k.tsum.at[1], k.trecv.at[1], k.t_send.at[1], k.t_recv.at[1], k.xn)
    k.arrived(k.trecv.at[1], k.t_recv.at[1])
    k.o_vec[...] = k.tsum[1] + k.trecv[1]


def feed_out(k):
    own, depth = k.own, k.depth

    def feed(j, row):
        a = k.hidden[pl.ds(row, 2 * own), :]
        for zz in range(k.lines):
            k.fbig[j * 2 * own : (j + 1) * 2 * own, zz * depth : (zz + 1) * depth] = dot(a, k.wd[zz])

    k.reduce_start(3, feed)
    k.reduce_diagonal(3)
    k.reduce_straight(3)

    def layer(rows, total):
        k.o_layer[rows, :] = (k.middle[rows, :] + total).astype(BF16)

    k.reduce_finish(3, layer)
    for copy in k.rs_sends:
        copy.wait_send()


def finish(k):
    y, z, rows, depth, qc, fc = k.y, k.z, k.rows, k.depth, k.qc, k.fc
    away = 1 - y
    places = k.lines - 1
    tile = 64
    stores = []

    def store(src, dst):
        copy = pltpu.make_async_copy(src, dst, k.stores.at[len(stores)])
        copy.start()
        stores.append(copy)

    def by_columns(m, send, recv, stage_row, out):
        n = fc if m == 4 else qc
        mine = pl.ds(stage_row, n)
        k.part_land(m)

        @pl.loop(0, n // tile)
        def _(i):
            some = pl.ds(pl.multiple_of(i * tile, tile), tile)
            source = k.gd if m == 4 else k.wo
            total = source[z, some, :].astype(F32)
            for p in range(places):
                total = total + k.h2[some, k.place(m, p)[1]].astype(F32)
            low, high = total[:, 0:rows], total[:, rows : 2 * rows]
            stage = pl.ds(pl.multiple_of(stage_row + i * tile, tile), tile)
            k.fbig[stage, 0:rows] = jnp.where(y == 0, low, high)
            send[some, :] = jnp.where(y == 0, high, low).astype(BF16)

        k.send(send, recv, k.h_send.at[m, 0], k.h_recv.at[m, 0], k.yn)
        store(k.fbig.at[mine, pl.ds(0, k.rpad)], out.at[pl.ds(pl.multiple_of(y * n, 8), n)])

        def later():
            k.arrived(recv, k.h_recv.at[m, 0])
            k.fbig[mine, 256 : 256 + rows] = recv[...].astype(F32)
            store(
                k.fbig.at[mine, pl.ds(256, k.rpad)], out.at[pl.ds(pl.multiple_of(away * n, 8), n)]
            )

        return later

    def by_rows(m, lead, send, recv, stage_row, stage_lane, out):
        n = qc if m == 0 else fc

        def row_sum(first, i):
            at = pl.multiple_of(first + i * tile, tile)
            own = pl.ds(pl.multiple_of(z * depth + at, tile), tile)
            total = (k.wq if m == 0 else k.wg)[lead, own, 0:n].astype(F32)
            for p in range(places):
                place_rows, lanes = k.place(m, p)
                start = lanes.start + (lead * qc if m == 0 else 0)
                came = pl.ds(pl.multiple_of(place_rows.start + at, tile), tile)
                total = total + k.h2[came, start : start + n].astype(F32)
            return total

        def put(i, side, value):
            into = pl.ds(pl.multiple_of(stage_row + i * tile, tile), tile)

            @pl.when(side == 0)
            def _():
                k.fbig[into, stage_lane : stage_lane + n] = value

            @pl.when(side == 1)
            def _():
                k.fbig[into, stage_lane + n : stage_lane + 2 * n] = value

        @pl.loop(0, rows // tile)
        def _(i):
            send[pl.ds(pl.multiple_of(i * tile, tile), tile), 0:n] = row_sum(
                away * rows, i
            ).astype(BF16)

        k.send(send, recv, k.h_send.at[m, lead], k.h_recv.at[m, lead], k.yn)

        @pl.loop(0, rows // tile)
        def _(i):
            put(i, y, row_sum(y * rows, i))

        def later():
            k.arrived(recv, k.h_recv.at[m, lead])

            @pl.loop(0, rows // tile)
            def _(i):
                put(i, away, recv[pl.ds(pl.multiple_of(i * tile, tile), tile), 0:n].astype(F32))

            store(k.fbig.at[pl.ds(stage_row, rows), pl.ds(stage_lane, 2 * n)], out)

        return later

    later = [by_columns(4, k.sdown.at[0], k.sdown.at[1], 0, k.o_down)]
    for m in (2, 3):
        i = m - 2
        k.part_land(m)
        later.append(by_rows(m, i, k.gu_away.at[i], k.y_gu.at[i], i * 256, 512, k.o_gu.at[i]))
    later.append(by_columns(1, k.sout.at[0], k.sout.at[1], k.tokens - 320, k.o_out))
    for last in later:
        last()
    k.flush()
    k.part_land(0)
    later = [
        by_rows(
            0,
            i,
            k.gu_away.at[0, :, pl.ds(i * qc, qc)],
            k.yrecv_q.at[i],
            512,
            512 + 2 * qc * i,
            k.o_qkv.at[i],
        )
        for i in range(3)
    ]
    for last in later:
        last()
    for copy in stores:
        copy.wait()


def kernel(names, sizes, *refs):
    k = Layer(sizes, dict(zip(names, refs)))
    forward(k)
    backward(k)
    vectors(k)
    feed_out(k)
    finish(k)
    k.flush()
    k.line_flush(4)
    for m in range(5):
        k.part_flush(m)


def layer_call(sizes, inputs):
    s = sizes
    lines, width, own, qc, fc, fpad, rows, depth, tokens = (
        s[n] for n in ("lines", "width", "own", "qc", "fc", "fpad", "rows", "depth", "tokens")
    )
    groups = 2 * lines
    small = max(qc, rows)
    vm = dict(
        wq=((3, width, qc), BF16),
        wo=((lines, qc, depth), BF16),
        wg=((2, width, fpad), BF16),
        wd=((lines, fc, depth), BF16),
        gd=((lines, fc, depth), BF16),
        h1=((tokens, width), BF16),
        h2=((tokens, width), BF16),
        og=((tokens, width), BF16),
        qkv=((3, tokens, qc), BF16),
        mixed=((tokens, qc), BF16),
        hidden=((tokens, fc), BF16),
        by_gate=((tokens, fc), BF16),
        by_up=((tokens, fc), BF16),
        middle=((own, width), F32),
        gmid=((own, width), F32),
        gains=((4, width), F32),
        fbig=((tokens, width), F32),
        csend=((4, own, width), BF16),
        crecv=((4, own, width), BF16),
        hrecv=((2, own, width), BF16),
        dvia=((2, own // 2, width), BF16),
        relay_q=((3, depth, qc), BF16),
        relay_g=((2, depth, fpad), BF16),
        gu_away=((2, rows, fpad), BF16),
        y_gu=((2, rows, fpad), BF16),
        sout=((2, qc, rows), BF16),
        sdown=((2, fc, rows), BF16),
        yrecv_q=((3, rows, qc), BF16),
        small=((groups, 8, 2 * qc), F32),
        tab=((tokens, 128), F32),
        segrow=((2, 8, s["length"]), F32),
        vecs=((4, width), F32),
        bsum=((2, qc), F32),
        vsend=((groups, 8, small), F32),
        vrecv=((groups, 8, small), F32),
        tsum=((2, 8, small), F32),
        trecv=((2, 8, small), F32),
    )
    sems = dict(
        ag_send=(4, 9),
        ag_recv=(4, 9),
        rs_send=(4, 8),
        rs_recv=(4, 8),
        z_send=(5, lines),
        z_recv=(5, lines),
        yx_send=(7,),
        yx_recv=(7,),
        sm_send=(groups - 1,),
        sm_recv=(groups,),
        g_send=(5, lines - 1),
        g_recv=(5, lines),
        g_relay=(5,),
        g_load=(lines - 1, 3),
        h_send=(5, 3),
        h_recv=(5, 3),
        v_send=(groups,),
        v_recv=(groups,),
        t_send=(2,),
        t_recv=(2,),
        loads=(5,),
        stores=(9,),
    )
    outs = dict(
        o_layer=((own, width), BF16, pltpu.VMEM),
        o_input=((own, width), BF16, pltpu.VMEM),
        o_vec=((8, small), F32, pltpu.VMEM),
        o_bias=((8, 2 * qc), F32, pltpu.VMEM),
        o_qkv=((3, rows, 2 * qc), F32, pl.ANY),
        o_out=((2 * qc, s["rpad"]), F32, pl.ANY),
        o_gu=((2, rows, 2 * fc), F32, pl.ANY),
        o_down=((2 * fc, s["rpad"]), F32, pl.ANY),
        r_q=((lines, 3, depth, qc), BF16, pl.ANY),
        r_o=((lines, qc, depth), BF16, pl.ANY),
        r_g=((lines, depth, fpad), BF16, pl.ANY),
        r_u=((lines, depth, fpad), BF16, pl.ANY),
        r_d=((lines, fc, depth), BF16, pl.ANY),
    )
    in_vm = ("in_res", "in_og", "in_tab", "in_seg", "in_small")
    names = list(inputs) + list(outs) + list(vm) + list(sems) + ["free"]
    results = pl.pallas_call(
        functools.partial(kernel, names, sizes),
        out_shape=[jax.ShapeDtypeStruct(a, d) for a, d, _ in outs.values()],
        in_specs=[
            pl.BlockSpec(memory_space=pltpu.VMEM if n in in_vm else pl.ANY) for n in inputs
        ],
        out_specs=[pl.BlockSpec(memory_space=m) for _, _, m in outs.values()],
        scratch_shapes=[pltpu.VMEM(*v) for v in vm.values()]
        + [pltpu.SemaphoreType.DMA(v) for v in sems.values()]
        + [pltpu.SemaphoreType.REGULAR],
        compiler_params=pltpu.CompilerParams(
            collective_id=1, has_side_effects=True, vmem_limit_bytes=63 * 2**20
        ),
    )(*inputs.values())
    return dict(zip([n[2:] for n in outs], results))


def prepare(lines, segment_ids, qkv_weight, qkv_bias, norm_gains, norm_biases):
    groups = 2 * lines
    f = lax.axis_index("z") * 2 + lax.axis_index("y")
    segments = segment_ids[0]
    table = tables(segments)
    seg_row = jnp.broadcast_to(segments.astype(F32)[None, :], (8, segments.shape[0]))
    width = qkv_weight.shape[2]
    two, heads, dims = qkv_bias.shape
    placed = lax.dynamic_update_slice(
        jnp.zeros((two, heads, groups, dims), F32), qkv_bias.astype(F32)[:, :, None, :], (0, 0, f, 0)
    ).reshape(two, width)
    params = jnp.concatenate([norm_gains, norm_biases], axis=0).astype(F32)
    params = jnp.pad(params, ((0, 0), (0, width - params.shape[1])))
    small = jnp.concatenate([params, placed, jnp.zeros((2, width), F32)], axis=0)
    return table, seg_row, small


def shards(
    lines,
    residual,
    segment_ids,
    qkv_weight,
    qkv_bias,
    out_weight,
    gate_up_weight,
    down_weight,
    norm_gains,
    norm_biases,
    out_grad,
):
    rows = qkv_weight.shape[1]
    qc = qkv_weight.shape[2] // 2
    fc = gate_up_weight.shape[2] // 2
    length = segment_ids.shape[1]
    table, seg_row, small = prepare(
        lines, segment_ids, qkv_weight, qkv_bias, norm_gains, norm_biases
    )
    sizes = dict(
        lines=lines,
        own=residual.shape[0],
        length=length,
        tokens=2 * length,
        width=residual.shape[1],
        rows=rows,
        depth=2 * rows,
        qc=qc,
        fc=fc,
        fpad=-(-fc // 128) * 128,
        rpad=-(-rows // 128) * 128,
    )
    r = layer_call(
        sizes,
        dict(
            in_res=residual,
            in_og=out_grad,
            in_tab=table,
            in_seg=seg_row,
            in_small=small,
            in_qkv=qkv_weight,
            in_out=out_weight,
            in_gu=gate_up_weight,
            in_down=down_weight,
        ),
    )
    f = lax.axis_index("z") * 2 + lax.axis_index("y")
    two, heads, dims = qkv_bias.shape
    bias = r["bias"][4:6].reshape(two, heads, 2 * lines, dims)
    bias = lax.dynamic_index_in_dim(bias, f, 2, keepdims=False)
    return (
        r["layer"],
        r["input"],
        r["qkv"],
        bias,
        r["out"][:, 0:rows],
        r["gu"],
        r["down"][:, 0:rows],
        r["vec"][0:2, 0:rows],
        r["vec"][2:4, 0:rows],
    )


def solution(mesh):
    groups, tp = mesh.shape["fsdp"], mesh.shape["tp"]
    lines = groups // 2
    cube = Mesh(mesh.devices.reshape(lines, 2, tp), ("z", "y", "tp"))
    fsdp = ("z", "y")
    token = P(("z", "y", "tp"), None)
    placed = (
        token,
        P(fsdp, None),
        P(None, fsdp, "tp"),
        P(None, "tp", fsdp),
        P("tp", fsdp),
        P(None, fsdp, "tp"),
        P("tp", fsdp),
        P(None, fsdp),
        P(None, fsdp),
        token,
    )
    return jax.shard_map(
        functools.partial(shards, lines),
        mesh=cube,
        in_specs=placed,
        out_specs=(
            token,
            token,
            P(None, fsdp, "tp"),
            P(None, "tp", fsdp),
            P("tp", fsdp),
            P(None, fsdp, "tp"),
            P("tp", fsdp),
            P(None, fsdp),
            P(None, fsdp),
        ),
        check_vma=False,
    )
```

```python
import functools
import math

import jax
import jax.numpy as jnp
from jax import lax
from jax.experimental import pallas as pl
from jax.experimental.pallas import tpu as pltpu
from jax.sharding import Mesh
from jax.sharding import PartitionSpec as P

HEAD = 64
ROT = 16
EPSILON = 1e-05
MASKED = -1e30
ROPE_BASE = 10000.0
F32 = jnp.float32
BF16 = jnp.bfloat16
MESH = pl.DeviceIdType.MESH
LSE = 100
NN = (((1,), (0,)), ((), ()))
NT = (((1,), (1,)), ((), ()))
TN = (((0,), (0,)), ((), ()))
SCALE = 1.0 / math.sqrt(HEAD)


def dot(a, b, dims=NN):
    return lax.dot_general(a, b, dims, preferred_element_type=F32)


def tables(segments):
    length = segments.shape[0]
    positions = jnp.arange(length, dtype=jnp.int32)
    starts_here = jnp.concatenate([jnp.ones((1,), jnp.bool_), segments[1:] != segments[:-1]])
    begins = lax.cummax(jnp.where(starts_here, positions, 0), axis=0)
    offsets = (positions - begins).astype(F32)
    half_rot = ROT // 2
    frequency = ROPE_BASE ** (-(jnp.arange(half_rot, dtype=F32) * 2.0 / ROT))
    angles = offsets[:, None] * frequency[None, :]
    cos, sin = jnp.cos(angles), jnp.sin(angles)
    seg = segments.astype(F32)
    return jnp.concatenate(
        [
            cos,
            cos,
            jnp.ones((length, HEAD - ROT), F32),
            -sin,
            sin,
            jnp.zeros((length, 32 - ROT), F32),
            seg[:, None],
            jnp.zeros((length, 31), F32),
        ],
        axis=1,
    )


class Layer:
    def __init__(self, sizes, refs):
        self.__dict__.update(sizes)
        self.__dict__.update(refs)
        self.z, self.y, self.t = (lax.axis_index(a) for a in ("z", "y", "tp"))
        self.core = lax.rem(self.t, 2)
        self.x = lax.div(self.t, 2)
        self.sib = (self.z, self.y, self.t + 1 - 2 * self.core)
        self.xn = (self.z, self.y, lax.rem(self.t + 2, 4))
        self.yn = (self.z, 1 - self.y, self.t)
        self.is_end = (self.z == 0) | (self.z == 3)
        self.sends = []

    def remote(self, src, dst, ssem, rsem, to):
        return pltpu.make_async_remote_copy(
            src_ref=src, dst_ref=dst, send_sem=ssem, recv_sem=rsem, device_id=to, device_id_type=MESH
        )

    def send(self, src, dst, ssem, rsem, to):
        copy = self.remote(src, dst, ssem, rsem, to)
        copy.start()
        self.sends.append(copy)

    def arrived(self, dst, rsem):
        self.remote(dst, dst, rsem, rsem, self.sib).wait_recv()

    def flush(self):
        for copy in self.sends:
            copy.wait_send()
        self.sends = []

    def chip_rows(self, y, x):
        return pl.multiple_of((y * 2 + x) * 2 * self.own, 2 * self.own)

    def chips(self):
        y, x = self.y, self.x
        return [
            self.chip_rows(1 - y, 1 - x),
            self.chip_rows(1 - y, x),
            self.chip_rows(y, 1 - x),
            self.chip_rows(y, x),
        ]

    def gather_start(self, u, buf):
        own, c = self.own, self.core
        mine = buf.at[pl.ds(pl.multiple_of(self.chips()[3] + c * own, own), own)]
        ss, rs = self.ag_send, self.ag_recv
        self.send(mine, mine, ss.at[u, 0], rs.at[u, 0], self.sib)
        self.send(mine, mine, ss.at[u, 1], rs.at[u, 1], self.xn)
        self.send(mine, mine, ss.at[u, 2], rs.at[u, 2], self.yn)

    def gather_relay(self, u, buf):
        own, c = self.own, self.core
        half = own // 2
        d, yr, xr, s = self.chips()
        ss, rs = self.ag_send, self.ag_recv

        def part(base, off, n):
            return buf.at[pl.ds(pl.multiple_of(base + c * own + off, half), n)]

        bx, by = part(xr, 0, own), part(yr, 0, own)
        self.arrived(bx, rs.at[u, 1])
        self.send(part(xr, 0, half), part(xr, 0, half), ss.at[u, 3], rs.at[u, 3], self.yn)
        self.send(bx, bx, ss.at[u, 4], rs.at[u, 4], self.sib)
        self.arrived(by, rs.at[u, 2])
        self.send(part(yr, half, half), part(yr, half, half), ss.at[u, 5], rs.at[u, 5], self.xn)
        self.send(by, by, ss.at[u, 6], rs.at[u, 6], self.sib)

    def gather_last(self, u, buf):
        own, c = self.own, self.core
        half = own // 2
        d = self.chips()[0]
        ss, rs = self.ag_send, self.ag_recv

        def part(off):
            return buf.at[pl.ds(pl.multiple_of(d + c * own + off, half), half)]

        self.arrived(part(0), rs.at[u, 3])
        self.send(part(0), part(0), ss.at[u, 7], rs.at[u, 7], self.sib)
        self.arrived(part(half), rs.at[u, 5])
        self.send(part(half), part(half), ss.at[u, 8], rs.at[u, 8], self.sib)

    def gather_wait(self, u, buf):
        own, c = self.own, self.core
        half = own // 2
        d, yr, xr, s = self.chips()
        rs = self.ag_recv

        def part(base, off, n):
            return buf.at[pl.ds(pl.multiple_of(base + (1 - c) * own + off, half), n)]

        self.arrived(part(s, 0, own), rs.at[u, 0])
        self.arrived(part(xr, 0, own), rs.at[u, 4])
        self.arrived(part(yr, 0, own), rs.at[u, 6])
        self.arrived(part(d, 0, half), rs.at[u, 7])
        self.arrived(part(d, half, half), rs.at[u, 8])

    def reduce_start(self, u, compute):
        own, c = self.own, self.core
        if u > 0:
            pl.semaphore_wait(self.free, 3)
            for copy in self.rs_sends:
                copy.wait_send()
        self.rs_sends = []
        self.core_sends = []
        for j, row in enumerate(self.chips()):
            compute(j, row)
            there = pl.ds(pl.multiple_of(j * 2 * own + (1 - c) * own, own), own)
            self.csend[j] = self.fbig[there, :].astype(BF16)
            copy = self.remote(
                self.csend.at[j], self.crecv.at[j], self.rs_send.at[u, j], self.rs_recv.at[u, j], self.sib
            )
            copy.start()
            self.core_sends.append(copy)

    def reduce_send(self, *what):
        copy = self.remote(*what)
        copy.start()
        self.rs_sends.append(copy)

    def reduce_mine(self, j, at=0, rows=None):
        own, c = self.own, self.core
        rows = own if rows is None else rows
        return self.fbig[pl.ds(pl.multiple_of(j * 2 * own + c * own + at, rows), rows), :]

    def reduce_diagonal(self, u):
        half = self.own // 2
        ss, rs = self.rs_send, self.rs_recv
        self.arrived(self.crecv.at[0], rs.at[u, 0])
        self.core_sends[0].wait_send()
        self.csend[0] = (self.reduce_mine(0) + self.crecv[0].astype(F32)).astype(BF16)
        first, second = pl.ds(0, half), pl.ds(half, half)
        self.reduce_send(self.csend.at[0, first], self.dvia.at[0], ss.at[u, 4], rs.at[u, 4], self.xn)
        self.reduce_send(self.csend.at[0, second], self.dvia.at[1], ss.at[u, 5], rs.at[u, 5], self.yn)

    def reduce_straight(self, u):
        own, half = self.own, self.own // 2
        ss, rs = self.rs_send, self.rs_recv
        for j, mixes, to in ((1, 0, self.yn), (2, 1, self.xn)):
            self.arrived(self.crecv.at[j], rs.at[u, j])
            self.core_sends[j].wait_send()
            for h in (1 - mixes, mixes):
                total = self.reduce_mine(j, h * half, half) + self.crecv[j, h * half : (h + 1) * half].astype(F32)
                if h == mixes:
                    self.arrived(self.dvia.at[j - 1], rs.at[u, 3 + j])
                    total = total + self.dvia[j - 1].astype(F32)
                self.csend[j, h * half : (h + 1) * half] = total.astype(BF16)
            self.reduce_send(self.csend.at[j], self.hrecv.at[j - 1], ss.at[u, 5 + j], rs.at[u, 5 + j], to)

    def reduce_finish(self, u, body):
        rs = self.rs_recv
        self.arrived(self.crecv.at[3], rs.at[u, 3])
        self.arrived(self.hrecv.at[0], rs.at[u, 6])
        self.arrived(self.hrecv.at[1], rs.at[u, 7])
        tile = 32

        @pl.loop(0, self.own // tile)
        def _(n):
            at = pl.multiple_of(n * tile, tile)
            rows = pl.ds(at, tile)
            total = self.reduce_mine(3, at, tile) + self.crecv[3, rows, :].astype(F32)
            total = total + self.hrecv[0, rows, :].astype(F32) + self.hrecv[1, rows, :].astype(F32)
            body(rows, total)

        self.core_sends[3].wait_send()
        if u < 3:
            for to in (self.sib, self.xn, self.yn):
                pl.semaphore_signal(self.free, inc=1, device_id=to, device_id_type=MESH)

    def item(self, m, zz):
        rows = pl.ds(pl.multiple_of(zz * self.depth, self.depth), self.depth)
        if m == 0:
            return self.wq.at[:, rows]
        if m == 1:
            return self.wo.at[zz]
        if m == 2:
            return self.wg.at[rows]
        return self.wd.at[zz]

    def role(self, at_end, in_middle):
        return jnp.where(self.is_end, at_end, in_middle)

    def roles(self):
        z = self.z
        low = z == 0
        return dict(
            near=self.role(jnp.where(low, 1, 2), 3 * (z - 1)),
            second=self.role(jnp.where(low, 2, 1), 3 - z),
            far=self.role(3 - z, 3 * (2 - z)),
        )

    def line_copy(self, m, zz, i, to):
        return self.remote(
            self.item(m, zz),
            self.item(m, zz),
            self.z_send.at[m, i],
            self.z_recv.at[m, zz],
            (to, self.y, self.t),
        )

    def line_start(self, m):
        z, n = self.z, self.lines
        if n != 4:
            for step in range(1, n):
                self.line_copy(m, z, step, lax.rem(z + step, n)).start()
            return
        r = self.roles()
        one, two = (r["second"], r["near"]) if m < 2 else (r["near"], r["second"])
        self.line_copy(m, z, 1, self.role(one, r["near"])).start()
        self.line_copy(m, z, 2, self.role(two, r["far"])).start()

        @pl.when(jnp.logical_not(self.is_end))
        def _():
            self.line_copy(m, z, 3, r["second"]).start()

    def line_relay(self, m):
        if self.lines != 4:
            return

        @pl.when(jnp.logical_not(self.is_end))
        def _():
            r = self.roles()
            self.arrived(self.item(m, r["far"]), self.z_recv.at[m, r["far"]])
            self.line_copy(m, r["far"], 0, r["near"]).start()

    def line_flush(self, m):
        z, n = self.z, self.lines
        for step in range(1, 3 if n == 4 else n):
            self.line_copy(m, z, step, z).wait_send()
        if n == 4:

            @pl.when(jnp.logical_not(self.is_end))
            def _():
                self.line_copy(m, z, 3, z).wait_send()
                self.line_copy(m, z, 0, z).wait_send()

    def line_order(self, m, s):
        z, n = self.z, self.lines
        if s == 0:
            return z
        if n != 4:
            return lax.rem(z + s, n)
        r = self.roles()
        if s == 3:
            return self.role(r["far"], r["second"])
        if s == 1:
            return self.role(r["near"], r["far"] if m < 2 else r["near"])
        return self.role(r["second"], r["near"] if m < 2 else r["far"])

    def line_wait(self, m, s):
        zz = self.line_order(m, s)
        if s == 0:
            return zz

        def wait():
            self.arrived(self.item(m, zz), self.z_recv.at[m, zz])

        if self.lines == 4 and s == (1 if m < 2 else 2):
            pl.when(self.is_end)(wait)
        else:
            wait()
        return zz

    def part(self, m, zz):
        return self.gd.at[zz] if m == 3 else self.item(m, zz)

    def relay(self, m):
        return (self.relay_q, self.relay_o, self.relay_g, self.relay_d)[m]

    def landing(self, m):
        return (self.r_q, self.r_o, self.r_g, self.r_d)[m]

    def part_order(self, i):
        n = self.lines
        if i == n - 1:
            return self.z
        if n != 4:
            return lax.rem(self.z + i + 1, n)
        r = self.roles()
        return (r["far"], r["second"], r["near"])[i]

    def part_copy(self, m, zz, i):
        return self.remote(
            self.part(m, zz),
            self.landing(m).at[self.z],
            self.g_send.at[m, i],
            self.g_recv.at[m, self.z],
            (zz, self.y, self.t),
        )

    def far_send(self, m, src):
        self.remote(
            src,
            self.relay(m),
            self.g_send.at[m, 0],
            self.g_relay.at[m],
            (self.roles()["near"], self.y, self.t),
        ).start()

    def part_send(self, m, i, far_sent=False):
        zz = self.part_order(i)
        if self.lines != 4 or i > 0:
            self.part_copy(m, zz, i).start()
        elif not far_sent:

            @pl.when(self.is_end)
            def _():
                self.far_send(m, self.part(m, zz))

    def part_relay(self, m):
        if self.lines != 4:
            return

        @pl.when(jnp.logical_not(self.is_end))
        def _():
            zz = self.part_order(0)
            self.arrived(self.relay(m), self.g_relay.at[m])
            mine, came = self.part(m, zz), self.relay(m)
            tile = 64

            @pl.loop(0, mine.shape[-2] // tile)
            def _(n):
                rows = pl.ds(pl.multiple_of(n * tile, tile), tile)
                at = (slice(None), rows) if len(mine.shape) == 3 else (rows,)
                mine[at] = (mine[at].astype(F32) + came[at].astype(F32)).astype(BF16)

            self.part_copy(m, zz, 0).start()

    def part_flush(self, m):
        for i in range(self.lines - 1):
            self.part_copy(m, self.z, i).wait_send()

    def place(self, m, p):
        if m in (1, 3):
            return self.h2, 0, p * self.depth
        fit = self.tokens // self.depth
        return (self.h2, self.h1)[p // fit], (p % fit) * self.depth, 0

    def part_slot(self, p):
        n = self.lines
        if n != 4:
            return lax.rem(self.z + p + 1, n)
        r = self.roles()
        return (r["near"], self.role(r["second"], r["far"]), self.role(r["far"], r["second"]))[p]

    def part_land(self, m):
        widths = (self.qc, self.depth, 2 * self.fc, self.depth)
        rows = (self.depth, self.qc, self.depth, self.fc)[m]
        parts = 3 if m == 0 else 1

        def copies(p):
            buf, row, lane = self.place(m, p)
            src = self.landing(m).at[self.part_slot(p)]
            for j in range(parts):
                into = buf.at[pl.ds(row, rows), pl.ds(lane + j * widths[m], widths[m])]
                yield pltpu.make_async_copy(src.at[j] if m == 0 else src, into, self.g_load.at[p, j])

        def begin(p):
            slot = self.part_slot(p)
            self.arrived(self.landing(m).at[slot], self.g_recv.at[m, slot])
            for copy in copies(p):
                copy.start()

        def end(p):
            for copy in copies(p):
                copy.wait()

        middle = jnp.logical_not(self.is_end)
        for p in range(self.lines - 1):
            if self.lines == 4 and p == 2:
                pl.when(middle)(functools.partial(begin, p))

                @pl.when(self.is_end)
                def _():
                    buf, row, lane = self.place(m, p)
                    some = parts * widths[m]
                    buf[row : row + rows, lane : lane + some] = jnp.zeros((rows, some), BF16)

            else:
                begin(p)
        for p in range(self.lines - 1):
            if self.lines == 4 and p == 2:
                pl.when(middle)(functools.partial(end, p))
            else:
                end(p)

    def enter(self):
        z, y, t = self.z, self.y, self.t
        barrier = pltpu.get_barrier_semaphore()
        n = 2 * self.lines
        f = z * 2 + y
        others = []
        for step in range(1, n):
            g = lax.rem(f + step, n)
            others.append((lax.div(g, 2), lax.rem(g, 2), t))
        for to in others + [self.sib, self.xn]:
            pl.semaphore_signal(barrier, inc=1, device_id=to, device_id_type=MESH)
        pl.semaphore_wait(barrier, n + 1)
        return f, others

    def unit_rows(self, rows):
        mean = jnp.mean(rows, axis=-1, keepdims=True)
        centred = rows - mean
        factor = lax.rsqrt(jnp.mean(centred * centred, axis=-1, keepdims=True) + EPSILON)
        return centred * factor, factor

    def rope_tables(self, g):
        rows = pl.ds(pl.multiple_of(g * self.length, self.length), self.length)
        both = self.tab[rows, :]
        lane = lax.broadcasted_iota(jnp.int32, both.shape, 1)
        turned = pltpu.roll(both, 64, 1)
        cos = jnp.where(lane < 64, both, turned)
        sin = jnp.where(lane < 64, turned, both)
        dim = lax.rem(lane, HEAD)
        seg = self.tab[rows, 96:97]
        return cos, jnp.where(dim < ROT, sin, 0.0), dim, seg

    def turn(self, v, dim):
        ahead = pltpu.roll(v, 128 - ROT // 2, 1)
        behind = pltpu.roll(v, ROT // 2, 1)
        return jnp.where(dim < ROT // 2, ahead, jnp.where(dim < ROT, behind, 0.0))

    def masked(self, scores, seg, g, r0):
        rows, cols = scores.shape
        at = lax.broadcasted_iota(jnp.int32, scores.shape, 0) + r0
        key = lax.broadcasted_iota(jnp.int32, scores.shape, 1)
        seg_row = self.segrow[g, 0:1, 0:cols]
        return jnp.where((seg == seg_row) & (at >= key), scores * SCALE, MASKED)


def forward(k):
    own, length, tokens = k.own, k.length, 2 * k.length
    width, rows_f, depth = k.width, k.rows, k.depth
    c, y = k.core, k.y
    f, others = k.enter()
    loads = k.loads
    frows = pl.ds(pl.multiple_of(f * rows_f, rows_f), rows_f)
    nrows = pl.ds(pl.multiple_of((f + 1 - 2 * y) * rows_f, rows_f), rows_f)
    away = 1 - y
    raws = [pl.ds(i * rows_f, rows_f) for i in range(2)]
    local = [
        pltpu.make_async_copy(src, dst, loads.at[i])
        for i, (src, dst) in enumerate(
            (
                (k.in_qkv.at[:, :, pl.ds(pl.multiple_of(y * k.qc, k.qc), k.qc)], k.wq.at[:, frows]),
                (k.in_out.at[pl.ds(pl.multiple_of(y * k.qc, k.qc), k.qc)], k.sout.at[y]),
                (k.in_gu.at[0], k.og.at[raws[0], pl.ds(0, 2 * k.fc)]),
                (k.in_gu.at[1], k.og.at[raws[1], pl.ds(0, 2 * k.fc)]),
                (k.in_down.at[pl.ds(pl.multiple_of(y * k.fc, 16), k.fc)], k.sdown.at[y]),
            )
        )
    ]
    for copy in local:
        copy.start()
    k.small[f] = k.in_small[...]
    for i, to in enumerate(others):
        k.send(k.in_small, k.small.at[f], k.sm_send.at[i], k.sm_recv.at[f], to)
    k.send(
        k.in_qkv.at[:, :, pl.ds(pl.multiple_of(away * k.qc, k.qc), k.qc)],
        k.wq.at[:, frows],
        k.yx_send.at[2], k.yx_recv.at[2], k.yn,
    )
    k.send(
        k.in_out.at[pl.ds(pl.multiple_of(away * k.qc, k.qc), k.qc)],
        k.sout.at[y],
        k.yx_send.at[3], k.yx_recv.at[3], k.yn,
    )
    unit, _ = k.unit_rows(k.in_res[...].astype(F32))
    for step in range(1, len(others) + 1):
        g = lax.rem(f + step, len(others) + 1)
        k.arrived(k.small.at[g], k.sm_recv.at[g])
    for g in range(len(others) + 1):
        k.gains[:, g * rows_f : (g + 1) * rows_f] = k.small[g, 0:4, 0:rows_f]
    bias = k.small[0, 4:6, :]
    for g in range(1, len(others) + 1):
        bias = bias + k.small[g, 4:6, :]
    bias = jnp.where(y == 0, bias[:, 0 : k.qc], bias[:, k.qc : 2 * k.qc])
    at = k.chips()[3] + c * own
    mine_rows = pl.ds(pl.multiple_of(at, own), own)
    k.h1[mine_rows, :] = (unit * k.gains[0:1, :] + k.gains[2:3, :]).astype(BF16)
    k.gather_start(0, k.h1)
    local[2].wait()
    local[3].wait()
    for i in range(2):
        low, high = k.og[raws[i], 0 : k.fc], k.og[raws[i], k.fc : 2 * k.fc]
        k.wg[frows, i * k.fc : (i + 1) * k.fc] = jnp.where(y == 0, low, high)
        k.gu_away[:, i * k.fc : (i + 1) * k.fc] = jnp.where(y == 0, high, low)

    local[0].wait()
    k.arrived(k.wq.at[:, nrows], k.yx_recv.at[2])
    k.line_start(0)
    local[1].wait()
    k.arrived(k.sout.at[away], k.yx_recv.at[3])
    k.wo[k.z] = jnp.concatenate([k.sout[0], k.sout[1]], axis=1)
    k.line_start(1)
    k.gather_relay(0, k.h1)
    mine = pl.ds(pl.multiple_of(y * length, length), length)
    k.tab[mine, :] = k.in_tab[...]
    k.segrow[y] = k.in_seg[...]
    k.send(k.in_tab, k.tab.at[mine], k.yx_send.at[0], k.yx_recv.at[0], k.yn)
    k.send(k.in_seg, k.segrow.at[y], k.yx_send.at[1], k.yx_recv.at[1], k.yn)
    k.send(k.gu_away, k.wg.at[frows], k.yx_send.at[4], k.yx_recv.at[4], k.yn)
    k.send(
        k.in_down.at[pl.ds(pl.multiple_of(away * k.fc, 16), k.fc)],
        k.sdown.at[y],
        k.yx_send.at[5], k.yx_recv.at[5], k.yn,
    )
    k.gather_last(0, k.h1)
    k.gather_wait(0, k.h1)
    k.og[mine_rows, :] = k.in_og[...]
    k.gather_start(1, k.og)

    tile = 256

    def project(s):
        zz = k.line_wait(0, s)
        cols = pl.ds(pl.multiple_of(zz * depth, depth), depth)

        @pl.loop(0, tokens // tile)
        def _(i):
            rows = pl.ds(pl.multiple_of(i * tile, tile), tile)
            a = k.h1[rows, cols]
            for j in range(3):
                out = dot(a, k.wq[j, cols, :])
                into = pl.ds(j * k.qc, k.qc)
                if s == 0:
                    k.fbig[rows, into] = out
                else:
                    k.fbig[rows, into] += out

    def later_lines():
        k.line_start(2)
        k.line_start(3)

    k.line_relay(0)
    project(0)
    for s in range(1, k.lines - 1):
        project(s)
    k.arrived(k.wg.at[nrows], k.yx_recv.at[4])
    local[4].wait()
    k.arrived(k.sdown.at[away], k.yx_recv.at[5])
    k.wd[k.z] = jnp.concatenate([k.sdown[0], k.sdown[1]], axis=1)
    if k.lines == 4:
        pl.when(k.is_end)(later_lines)
    k.line_relay(1)
    if k.lines == 4:
        pl.when(jnp.logical_not(k.is_end))(later_lines)
    else:
        later_lines()
    project(k.lines - 1)

    k.gather_relay(1, k.og)
    k.arrived(k.tab.at[pl.ds(pl.multiple_of(away * length, length), length)], k.yx_recv.at[0])
    k.arrived(k.segrow.at[away], k.yx_recv.at[1])

    pairs = k.qc // 128
    block = 256

    @pl.loop(0, 2)
    def _(g):
        rows = pl.ds(pl.multiple_of(g * length, length), length)
        cos, sin, dim, seg = k.rope_tables(g)
        for p in range(pairs):
            into = pl.ds(p * 128, 128)

            def part(j):
                return k.fbig[rows, pl.ds(j * k.qc + p * 128, 128)]

            q = part(0) + bias[0:1, p * 128 : (p + 1) * 128]
            kk = part(1)
            k.qkv[0, rows, into] = (q * cos + k.turn(q, dim) * sin).astype(BF16)
            k.qkv[1, rows, into] = (kk * cos + k.turn(kk, dim) * sin).astype(BF16)
            k.qkv[2, rows, into] = (part(2) + bias[1:2, p * 128 : (p + 1) * 128]).astype(BF16)
            for r in range(0, length, block):
                some = pl.ds(pl.multiple_of(g * length + r, block), block)
                seen = pl.ds(pl.multiple_of(g * length, length), r + block)
                qb = k.qkv[0, some, into]
                kb = k.qkv[1, seen, into]
                vb = k.qkv[2, seen, into]
                low = lax.broadcasted_iota(jnp.int32, (block, 128), 1) < HEAD
                both = []
                marks = []
                for h in range(2):
                    mask = low if h == 0 else jnp.logical_not(low)
                    scores = dot(jnp.where(mask, qb, jnp.zeros_like(qb)), kb, NT)
                    scores = k.masked(scores, seg[r : r + block], g, r)
                    top = jnp.max(scores, axis=-1, keepdims=True)
                    e = jnp.exp(scores - top)
                    total = jnp.sum(e, axis=-1, keepdims=True)
                    probs = (e / total).astype(BF16)
                    both.append(dot(probs, vb))
                    marks.append(top + jnp.log(total))
                k.mixed[some, into] = jnp.where(low, both[0], both[1]).astype(BF16)
                at_lane = lax.broadcasted_iota(jnp.int32, (block, 128), 1)
                old = k.tab[some, :]
                old = jnp.where(at_lane == LSE + 2 * p, marks[0], old)
                k.tab[some, :] = jnp.where(at_lane == LSE + 2 * p + 1, marks[1], old)

    k.gather_last(1, k.og)
    for s in range(k.lines):
        k.line_wait(1, s)

    def out_rows(j, row):
        a = k.mixed[pl.ds(row, 2 * own), :]
        for zz in range(k.lines):
            k.fbig[j * 2 * own : (j + 1) * 2 * own, zz * depth : (zz + 1) * depth] = dot(a, k.wo[zz])

    k.reduce_start(0, out_rows)
    k.reduce_diagonal(0)
    k.reduce_straight(0)

    def second_norm(rows, total):
        middle = k.in_res[rows, :].astype(F32) + total
        k.middle[rows, :] = middle
        unit, _ = k.unit_rows(middle)
        into = pl.ds(pl.multiple_of(at + rows.start, 32), rows.size)
        k.h2[into, :] = (unit * k.gains[1:2, :] + k.gains[3:4, :]).astype(BF16)

    k.reduce_finish(0, second_norm)
    k.gather_start(2, k.h2)
    k.gather_wait(1, k.og)
    k.gather_relay(2, k.h2)
    k.gather_last(2, k.h2)
    k.gather_wait(2, k.h2)

    def gate_up(s):
        zz = k.line_wait(2, s)
        cols = pl.ds(pl.multiple_of(zz * depth, depth), depth)

        @pl.loop(0, tokens // tile)
        def _(n):
            rows = pl.ds(pl.multiple_of(n * tile, tile), tile)
            a = k.h2[rows, cols]
            for lane in range(0, 2 * k.fc, 512):
                into = pl.ds(lane, min(512, 2 * k.fc - lane))
                out = dot(a, k.wg[cols, into])
                if s == 0:
                    k.fbig[rows, into] = out
                else:
                    k.fbig[rows, into] += out

    gate_up(0)
    gate_up(1)
    k.line_relay(2)
    for s in range(2, k.lines - 1):
        gate_up(s)
    k.line_relay(3)
    gate_up(k.lines - 1)

    @pl.loop(0, tokens // 64)
    def _(n):
        rows = pl.ds(pl.multiple_of(n * 64, 64), 64)
        gate = k.fbig[rows, 0 : k.fc]
        up = k.fbig[rows, k.fc : 2 * k.fc]
        sig = 1.0 / (1.0 + jnp.exp(-gate))
        silu = gate * sig
        k.hidden[rows, :] = (silu * up).astype(BF16)
        k.by[rows, 0 : k.fc] = (up * sig * (1.0 + gate * (1.0 - sig))).astype(BF16)
        k.by[rows, k.fc : 2 * k.fc] = silu.astype(BF16)


def norm_back(k, which, grad, unit, factor):
    k.vecs[which : which + 1, :] += jnp.sum(grad * unit, axis=0, keepdims=True)
    k.vecs[which + 2 : which + 3, :] += jnp.sum(grad, axis=0, keepdims=True)
    scaled = grad * k.gains[which : which + 1, :]
    centred = scaled - jnp.mean(scaled, axis=-1, keepdims=True)
    return factor * (centred - unit * jnp.mean(scaled * unit, axis=-1, keepdims=True))


def weight_grads(k, m, block, far_sent=False):
    for i in range(k.lines):
        if i == 0 and far_sent and k.lines == 4:
            pl.when(jnp.logical_not(k.is_end))(lambda: block(k.part_order(0)))
        else:
            block(k.part_order(i))
        if i < k.lines - 1:
            k.part_send(m, i, far_sent)


def backward(k):
    own, length, tokens = k.own, k.length, k.tokens
    depth, fc, qc = k.depth, k.fc, k.qc
    c, y, z = k.core, k.y, k.z
    tile = 256
    at_own = k.chips()[3] + c * own
    k.vecs[...] = jnp.zeros_like(k.vecs)

    def down_block(zz):
        cols = pl.ds(pl.multiple_of(zz * depth, depth), depth)
        k.gd[zz] = dot(k.hidden[...], k.og[:, cols], TN).astype(BF16)

    weight_grads(k, 3, down_block)

    for s in range(k.lines):
        zz = k.line_wait(3, s)
        cols = pl.ds(pl.multiple_of(zz * depth, depth), depth)

        @pl.loop(0, tokens // tile)
        def _(n):
            rows = pl.ds(pl.multiple_of(n * tile, tile), tile)
            out = dot(k.og[rows, cols], k.wd[zz], NT)
            if s == 0:
                k.fbig[rows, 0:fc] = out
            else:
                k.fbig[rows, 0:fc] += out

    @pl.loop(0, tokens // 64)
    def _(n):
        rows = pl.ds(pl.multiple_of(n * 64, 64), 64)
        grad = k.fbig[rows, 0:fc]
        for lanes in (pl.ds(0, fc), pl.ds(fc, fc)):
            k.by[rows, lanes] = (grad * k.by[rows, lanes].astype(F32)).astype(BF16)

    def back_two(j, row):
        a = k.by[pl.ds(row, 2 * own), :]
        for n in range(0, k.width, 512):
            k.fbig[j * 2 * own : (j + 1) * 2 * own, n : n + 512] = dot(a, k.wg[pl.ds(n, 512), :], NT)

    def gate_block(zz, into=None):
        cols = pl.ds(pl.multiple_of(zz * depth, depth), depth)
        a = k.h2[:, cols]
        for lane in range(0, 2 * fc, 512):
            some = pl.ds(lane, min(512, 2 * fc - lane))
            out = dot(a, k.by[:, some], TN).astype(BF16)
            if into is None:
                k.wg[cols, some] = out
            else:
                into[:, some] = out

    if k.lines == 4:

        @pl.when(k.is_end)
        def _():
            gate_block(k.part_order(0), k.relay_g)
            k.far_send(2, k.relay_g)

    k.flush()
    k.reduce_start(1, back_two)
    k.reduce_diagonal(1)
    k.line_flush(2)
    weight_grads(k, 2, gate_block, True)
    k.reduce_straight(1)
    k.part_relay(3)

    def second_back(rows, total):
        unit, factor = k.unit_rows(k.middle[rows, :])
        back = norm_back(k, 1, total, unit, factor)
        grad_middle = k.in_og[rows, :].astype(F32) + back
        k.gmid[rows, :] = grad_middle
        into = pl.ds(pl.multiple_of(at_own + rows.start, 32), rows.size)
        k.og[into, :] = grad_middle.astype(BF16)

    k.reduce_finish(1, second_back)
    k.gather_start(3, k.og)
    k.gather_relay(3, k.og)
    k.gather_last(3, k.og)
    k.gather_wait(3, k.og)

    k.part_relay(2)
    @pl.loop(0, tokens // tile)
    def _(n):
        rows = pl.ds(pl.multiple_of(n * tile, tile), tile)
        out = dot(k.og[rows, 0:depth], k.wo[0], NT)
        for zz in range(1, k.lines):
            out = out + dot(k.og[rows, zz * depth : (zz + 1) * depth], k.wo[zz], NT)
        k.h2[rows, 0:qc] = out.astype(BF16)

    block = 256
    k.bsum[...] = jnp.zeros_like(k.bsum)

    @pl.loop(0, 2)
    def _(g):
        rows = pl.ds(pl.multiple_of(g * length, length), length)
        cos, sin, dim, seg = k.rope_tables(g)
        for p in range(qc // 128):
            into = pl.ds(p * 128, 128)
            for r in range(0, length, block):
                some = pl.ds(pl.multiple_of(g * length + r, block), block)
                seen = pl.ds(pl.multiple_of(g * length, length), r + block)
                qb = k.qkv[0, some, into]
                kb = k.qkv[1, seen, into]
                vb = k.qkv[2, seen, into]
                gb = k.h2[some, into]
                lane = lax.broadcasted_iota(jnp.int32, (block, 128), 1)
                low = lane < HEAD
                marks = k.tab[some, :]
                gq, gk, gv = [], [], []
                for h in range(2):
                    mask = low if h == 0 else jnp.logical_not(low)
                    qm = jnp.where(mask, qb, jnp.zeros_like(qb))
                    gm = jnp.where(mask, gb, jnp.zeros_like(gb))
                    mark = jnp.sum(jnp.where(lane == LSE + 2 * p + h, marks, 0.0), axis=1, keepdims=True)
                    scores = k.masked(dot(qm, kb, NT), seg[r : r + block], g, r)
                    probs = jnp.exp(scores - mark)
                    dp = dot(gm, vb, NT)
                    inner = jnp.sum(probs * dp, axis=-1, keepdims=True)
                    gs = (probs * (dp - inner)).astype(BF16)
                    gq.append(dot(gs, kb))
                    gk.append(dot(gs, qm, TN))
                    gv.append(dot(probs.astype(BF16), gm, TN))
                k.fbig[some, pl.ds(p * 128, 128)] = jnp.where(low, gq[0], gq[1]) * SCALE
                for j, v in ((1, (gk[0] + gk[1]) * SCALE), (2, gv[0] + gv[1])):
                    cols = pl.ds(j * qc + p * 128, 128)
                    if r > 0:
                        before = pl.ds(pl.multiple_of(g * length, length), r)
                        k.fbig[before, cols] += v[0:r]
                    k.fbig[some, cols] = v[r : r + block]
            for j in range(3):
                v = k.fbig[rows, pl.ds(j * qc + p * 128, 128)]
                if j < 2:
                    v = v * cos + k.turn(v * sin, dim)
                v = v.astype(BF16)
                k.qkv[j, rows, into] = v
                if j != 1:
                    half = j // 2
                    k.bsum[half : half + 1, into] += jnp.sum(v.astype(F32), axis=0, keepdims=True)

    def back_one(j, row):
        rows = pl.ds(row, 2 * own)
        parts = [k.qkv[i, rows, :] for i in range(3)]
        for n in range(0, k.width, 512):
            some = pl.ds(n, 512)
            out = dot(parts[0], k.wq[0, some, :], NT)
            for i in (1, 2):
                out = out + dot(parts[i], k.wq[i, some, :], NT)
            k.fbig[j * 2 * own : (j + 1) * 2 * own, n : n + 512] = out

    k.reduce_start(2, back_one)
    k.line_flush(0)
    k.line_flush(1)
    k.reduce_diagonal(2)

    def qkv_block(zz):
        cols = pl.ds(pl.multiple_of(zz * depth, depth), depth)
        for i in range(3):
            k.wq[i, cols, :] = dot(k.h1[:, cols], k.qkv[i], TN).astype(BF16)

    def out_block(zz):
        cols = pl.ds(pl.multiple_of(zz * depth, depth), depth)
        k.wo[zz] = dot(k.mixed[...], k.og[:, cols], TN).astype(BF16)

    weight_grads(k, 1, out_block)
    k.reduce_straight(2)
    weight_grads(k, 0, qkv_block)

    def first_back(rows, total):
        unit, factor = k.unit_rows(k.in_res[rows, :].astype(F32))
        back = norm_back(k, 0, total, unit, factor)
        k.o_input[rows, :] = (k.gmid[rows, :] + back).astype(BF16)

    k.reduce_finish(2, first_back)


def vectors_send(k):
    f = k.z * 2 + k.y
    n = 2 * k.lines
    rows = k.rows
    k.vsend[...] = jnp.zeros_like(k.vsend)
    for g in range(n):
        k.vsend[g, 0:4, 0:rows] = k.vecs[0:4, g * rows : (g + 1) * rows]
        k.vsend[g, 4:6, 0 : k.qc] = k.bsum[0:2, :]
    for step in range(1, n):
        g = lax.rem(f + step, n)
        k.send(
            k.vsend.at[g], k.vrecv.at[f], k.v_send.at[step], k.v_recv.at[f],
            (lax.div(g, 2), lax.rem(g, 2), k.t),
        )
    k.vrecv[f] = k.vsend[f]


def vectors(k):
    f = k.z * 2 + k.y
    n = 2 * k.lines
    for step in range(1, n):
        g = lax.rem(f + step, n)
        k.arrived(k.vrecv.at[g], k.v_recv.at[g])
    total = k.vrecv[0]
    sides = [k.vrecv[0], k.vrecv[1]]
    for g in range(1, n):
        total = total + k.vrecv[g]
        if g > 1:
            sides[g % 2] = sides[g % 2] + k.vrecv[g]
    k.o_bias[:, 0 : k.qc] = sides[0][:, 0 : k.qc]
    k.o_bias[:, k.qc : 2 * k.qc] = sides[1][:, 0 : k.qc]
    k.tsum[0] = total
    k.send(k.tsum.at[0], k.trecv.at[0], k.t_send.at[0], k.t_recv.at[0], k.sib)
    k.arrived(k.trecv.at[0], k.t_recv.at[0])
    k.tsum[1] = total + k.trecv[0]
    k.send(k.tsum.at[1], k.trecv.at[1], k.t_send.at[1], k.t_recv.at[1], k.xn)
    k.arrived(k.trecv.at[1], k.t_recv.at[1])
    k.o_vec[...] = k.tsum[1] + k.trecv[1]


def feed_out(k):
    own, depth = k.own, k.depth

    def feed(j, row):
        a = k.hidden[pl.ds(row, 2 * own), :]
        for zz in range(k.lines):
            k.fbig[j * 2 * own : (j + 1) * 2 * own, zz * depth : (zz + 1) * depth] = dot(a, k.wd[zz])

    k.reduce_start(3, feed)
    k.reduce_diagonal(3)
    k.reduce_straight(3)

    def layer(rows, total):
        k.o_layer[rows, :] = (k.middle[rows, :] + total).astype(BF16)

    k.reduce_finish(3, layer)
    for copy in k.rs_sends:
        copy.wait_send()


def finish(k):
    y, z, rows, depth, qc, fc = k.y, k.z, k.rows, k.depth, k.qc, k.fc
    away = 1 - y
    places = k.lines - 1
    tile = 64
    stores = []

    def store(src, dst):
        copy = pltpu.make_async_copy(src, dst, k.stores.at[len(stores)])
        copy.start()
        stores.append(copy)

    def by_columns(m, send, recv, stage_row, out):
        n = fc if m == 3 else qc
        mine = pl.ds(stage_row, n)
        k.part_land(m)

        @pl.loop(0, n // tile)
        def _(i):
            some = pl.ds(pl.multiple_of(i * tile, tile), tile)
            source = k.gd if m == 3 else k.wo
            total = source[z, some, :].astype(F32)
            for p in range(places):
                buf, _, lane = k.place(m, p)
                total = total + buf[some, lane : lane + depth].astype(F32)
            low, high = total[:, 0:rows], total[:, rows : 2 * rows]
            stage = pl.ds(pl.multiple_of(stage_row + i * tile, tile), tile)
            k.fbig[stage, 0:rows] = jnp.where(y == 0, low, high)
            send[some, :] = jnp.where(y == 0, high, low).astype(BF16)

        k.send(send, recv, k.h_send.at[m, 0], k.h_recv.at[m, 0], k.yn)
        store(k.fbig.at[mine, pl.ds(0, k.rpad)], out.at[pl.ds(pl.multiple_of(y * n, 8), n)])

        def later():
            k.arrived(recv, k.h_recv.at[m, 0])
            k.fbig[mine, 256 : 256 + rows] = recv[...].astype(F32)
            store(
                k.fbig.at[mine, pl.ds(256, k.rpad)], out.at[pl.ds(pl.multiple_of(away * n, 8), n)]
            )

        return later

    def by_rows(m, lead, send, recv, stages, out):
        n = qc if m == 0 else fc
        wide = qc if m == 0 else 2 * fc

        def row_sum(first, i):
            at = pl.multiple_of(first + i * tile, tile)
            own = pl.ds(pl.multiple_of(z * depth + at, tile), tile)
            total = (k.wq[lead, own, :] if m == 0 else k.wg[own, :]).astype(F32)
            for p in range(places):
                buf, row, lane = k.place(m, p)
                start = lane + lead * qc
                came = pl.ds(pl.multiple_of(row + at, tile), tile)
                total = total + buf[came, start : start + wide].astype(F32)
            return total

        def put(i, side, value):
            for j, (row, lane) in enumerate(stages):
                into = pl.ds(pl.multiple_of(row + i * tile, tile), tile)
                for at_y in range(2):

                    @pl.when(side == at_y)
                    def _():
                        k.fbig[into, lane + at_y * n : lane + (at_y + 1) * n] = value[
                            :, j * n : (j + 1) * n
                        ]

        @pl.loop(0, rows // tile)
        def _(i):
            some = pl.ds(pl.multiple_of(i * tile, tile), tile)
            send[some, :] = row_sum(away * rows, i).astype(BF16)

        k.send(send, recv, k.h_send.at[m, lead], k.h_recv.at[m, lead], k.yn)

        @pl.loop(0, rows // tile)
        def _(i):
            put(i, y, row_sum(y * rows, i))

        def later():
            k.arrived(recv, k.h_recv.at[m, lead])

            @pl.loop(0, rows // tile)
            def _(i):
                put(i, away, recv[pl.ds(pl.multiple_of(i * tile, tile), tile), :].astype(F32))

            for j, (row, lane) in enumerate(stages):
                store(k.fbig.at[pl.ds(row, rows), pl.ds(lane, 2 * n)], out[j])

        return later

    later = [by_columns(3, k.sdown.at[0], k.sdown.at[1], 0, k.o_down)]
    k.part_land(2)
    later.append(
        by_rows(
            2, 0, k.gu_away, k.y_gu, [(0, 512), (256, 512)], [k.o_gu.at[0], k.o_gu.at[1]]
        )
    )
    k.part_relay(1)
    k.part_relay(0)
    later.append(by_columns(1, k.sout.at[0], k.sout.at[1], k.tokens - 320, k.o_out))
    for last in later:
        last()
    k.flush()
    vectors(k)
    k.part_land(0)
    later = [
        by_rows(
            0,
            i,
            k.gu_away.at[:, pl.ds(i * qc, qc)],
            k.yrecv_q.at[i],
            [(512, 512 + 2 * qc * i)],
            [k.o_qkv.at[i]],
        )
        for i in range(3)
    ]
    for last in later:
        last()
    for copy in stores:
        copy.wait()


def kernel(names, sizes, *refs):
    k = Layer(sizes, dict(zip(names, refs)))
    forward(k)
    backward(k)
    vectors_send(k)
    feed_out(k)
    finish(k)
    k.flush()
    k.line_flush(3)
    for m in range(4):
        k.part_flush(m)


def layer_call(sizes, inputs):
    s = sizes
    lines, width, own, qc, fc, rows, depth, tokens = (
        s[n] for n in ("lines", "width", "own", "qc", "fc", "rows", "depth", "tokens")
    )
    groups = 2 * lines
    small = max(qc, rows)
    vm = dict(
        wq=((3, width, qc), BF16),
        wo=((lines, qc, depth), BF16),
        wg=((width, 2 * fc), BF16),
        wd=((lines, fc, depth), BF16),
        gd=((lines, fc, depth), BF16),
        h1=((tokens, width), BF16),
        h2=((tokens, width), BF16),
        og=((tokens, width), BF16),
        qkv=((3, tokens, qc), BF16),
        mixed=((tokens, qc), BF16),
        hidden=((tokens, fc), BF16),
        by=((tokens, 2 * fc), BF16),
        middle=((own, width), F32),
        gmid=((own, width), F32),
        gains=((4, width), F32),
        fbig=((tokens, width), F32),
        csend=((4, own, width), BF16),
        crecv=((4, own, width), BF16),
        hrecv=((2, own, width), BF16),
        dvia=((2, own // 2, width), BF16),
        relay_q=((3, depth, qc), BF16),
        relay_o=((qc, depth), BF16),
        relay_g=((depth, 2 * fc), BF16),
        relay_d=((fc, depth), BF16),
        gu_away=((rows, 2 * fc), BF16),
        y_gu=((rows, 2 * fc), BF16),
        sout=((2, qc, rows), BF16),
        sdown=((2, fc, rows), BF16),
        yrecv_q=((3, rows, qc), BF16),
        small=((groups, 8, 2 * qc), F32),
        tab=((tokens, 128), F32),
        segrow=((2, 8, s["length"]), F32),
        vecs=((4, width), F32),
        bsum=((2, qc), F32),
        vsend=((groups, 8, small), F32),
        vrecv=((groups, 8, small), F32),
        tsum=((2, 8, small), F32),
        trecv=((2, 8, small), F32),
    )
    sems = dict(
        ag_send=(4, 9),
        ag_recv=(4, 9),
        rs_send=(4, 8),
        rs_recv=(4, 8),
        z_send=(4, lines),
        z_recv=(4, lines),
        yx_send=(6,),
        yx_recv=(6,),
        sm_send=(groups - 1,),
        sm_recv=(groups,),
        g_send=(4, lines - 1),
        g_recv=(4, lines),
        g_relay=(4,),
        g_load=(lines - 1, 3),
        h_send=(4, 3),
        h_recv=(4, 3),
        v_send=(groups,),
        v_recv=(groups,),
        t_send=(2,),
        t_recv=(2,),
        loads=(5,),
        stores=(9,),
    )
    outs = dict(
        o_layer=((own, width), BF16, pltpu.VMEM),
        o_input=((own, width), BF16, pltpu.VMEM),
        o_vec=((8, small), F32, pltpu.VMEM),
        o_bias=((8, 2 * qc), F32, pltpu.VMEM),
        o_qkv=((3, rows, 2 * qc), F32, pl.ANY),
        o_out=((2 * qc, s["rpad"]), F32, pl.ANY),
        o_gu=((2, rows, 2 * fc), F32, pl.ANY),
        o_down=((2 * fc, s["rpad"]), F32, pl.ANY),
        r_q=((lines, 3, depth, qc), BF16, pl.ANY),
        r_o=((lines, qc, depth), BF16, pl.ANY),
        r_g=((lines, depth, 2 * fc), BF16, pl.ANY),
        r_d=((lines, fc, depth), BF16, pl.ANY),
    )
    in_vm = ("in_res", "in_og", "in_tab", "in_seg", "in_small")
    names = list(inputs) + list(outs) + list(vm) + list(sems) + ["free"]
    results = pl.pallas_call(
        functools.partial(kernel, names, sizes),
        out_shape=[jax.ShapeDtypeStruct(a, d) for a, d, _ in outs.values()],
        in_specs=[
            pl.BlockSpec(memory_space=pltpu.VMEM if n in in_vm else pl.ANY) for n in inputs
        ],
        out_specs=[pl.BlockSpec(memory_space=m) for _, _, m in outs.values()],
        scratch_shapes=[pltpu.VMEM(*v) for v in vm.values()]
        + [pltpu.SemaphoreType.DMA(v) for v in sems.values()]
        + [pltpu.SemaphoreType.REGULAR],
        compiler_params=pltpu.CompilerParams(
            collective_id=1, has_side_effects=True, vmem_limit_bytes=63 * 2**20
        ),
    )(*inputs.values())
    return dict(zip([n[2:] for n in outs], results))


def prepare(lines, segment_ids, qkv_weight, qkv_bias, norm_gains, norm_biases):
    groups = 2 * lines
    f = lax.axis_index("z") * 2 + lax.axis_index("y")
    segments = segment_ids[0]
    table = tables(segments)
    seg_row = jnp.broadcast_to(segments.astype(F32)[None, :], (8, segments.shape[0]))
    width = qkv_weight.shape[2]
    two, heads, dims = qkv_bias.shape
    placed = lax.dynamic_update_slice(
        jnp.zeros((two, heads, groups, dims), F32), qkv_bias.astype(F32)[:, :, None, :], (0, 0, f, 0)
    ).reshape(two, width)
    params = jnp.concatenate([norm_gains, norm_biases], axis=0).astype(F32)
    params = jnp.pad(params, ((0, 0), (0, width - params.shape[1])))
    small = jnp.concatenate([params, placed, jnp.zeros((2, width), F32)], axis=0)
    return table, seg_row, small


def shards(
    lines,
    residual,
    segment_ids,
    qkv_weight,
    qkv_bias,
    out_weight,
    gate_up_weight,
    down_weight,
    norm_gains,
    norm_biases,
    out_grad,
):
    rows = qkv_weight.shape[1]
    qc = qkv_weight.shape[2] // 2
    fc = gate_up_weight.shape[2] // 2
    length = segment_ids.shape[1]
    table, seg_row, small = prepare(
        lines, segment_ids, qkv_weight, qkv_bias, norm_gains, norm_biases
    )
    sizes = dict(
        lines=lines,
        own=residual.shape[0],
        length=length,
        tokens=2 * length,
        width=residual.shape[1],
        rows=rows,
        depth=2 * rows,
        qc=qc,
        fc=fc,
        rpad=-(-rows // 128) * 128,
    )
    r = layer_call(
        sizes,
        dict(
            in_res=residual,
            in_og=out_grad,
            in_tab=table,
            in_seg=seg_row,
            in_small=small,
            in_qkv=qkv_weight,
            in_out=out_weight,
            in_gu=gate_up_weight,
            in_down=down_weight,
        ),
    )
    f = lax.axis_index("z") * 2 + lax.axis_index("y")
    two, heads, dims = qkv_bias.shape
    bias = r["bias"][4:6].reshape(two, heads, 2 * lines, dims)
    bias = lax.dynamic_index_in_dim(bias, f, 2, keepdims=False)
    return (
        r["layer"],
        r["input"],
        r["qkv"],
        bias,
        r["out"][:, 0:rows],
        r["gu"],
        r["down"][:, 0:rows],
        r["vec"][0:2, 0:rows],
        r["vec"][2:4, 0:rows],
    )


def solution(mesh):
    groups, tp = mesh.shape["fsdp"], mesh.shape["tp"]
    lines = groups // 2
    cube = Mesh(mesh.devices.reshape(lines, 2, tp), ("z", "y", "tp"))
    fsdp = ("z", "y")
    token = P(("z", "y", "tp"), None)
    placed = (
        token,
        P(fsdp, None),
        P(None, fsdp, "tp"),
        P(None, "tp", fsdp),
        P("tp", fsdp),
        P(None, fsdp, "tp"),
        P("tp", fsdp),
        P(None, fsdp),
        P(None, fsdp),
        token,
    )
    return jax.shard_map(
        functools.partial(shards, lines),
        mesh=cube,
        in_specs=placed,
        out_specs=(
            token,
            token,
            P(None, fsdp, "tp"),
            P(None, "tp", fsdp),
            P("tp", fsdp),
            P(None, fsdp, "tp"),
            P("tp", fsdp),
            P(None, fsdp),
            P(None, fsdp),
        ),
        check_vma=False,
    )
```
